32 devices in a mesh: row: 4 (over z), col: 8 (over y, x, core).
Axes of the slice: x: 2, y: 2, z: 4, core: 2. Of those that a mesh axis runs over, the one named last changes fastest.
Arguments:
- activations: bfloat16 [96, 48, 3072], P('row', None, 'col'), may hold values from -30 to 30
- cotangent: bfloat16 [96, 48, 3072], P('row', None, 'col'), may hold values from -6 to 6
- kernel: float32 [7, 7, 3072], P(None, None, 'col'), may hold values from -0.875 to 0.875
- ln_gain: float32 [3072], replicated, may hold values from 0.25 to 1.75
- ln_bias: float32 [3072], replicated, may hold values from -3 to 3
- w_expand: bfloat16 [3072, 12288], P('row', 'col'), may hold values from -0.5 to 0.5
- b_expand: float32 [12288], P('col'), may hold values from -3 to 3
- w_reduce: bfloat16 [12288, 3072], P('col', 'row'), may hold values from -0.078125 to 0.078125
- b_reduce: float32 [3072], P('col'), may hold values from -3 to 3
- layer_scale: float32 [3072], P('col'), may hold values from 0.3 to 1.5
Outputs:
- block_out: bfloat16 [96, 48, 3072], P('row', None, 'col')
- grad_input: bfloat16 [96, 48, 3072], P('row', None, 'col')
The draws below stay inside these ranges and needn't reach their ends.
All inputs are finite; a program needn't handle non-finite values.
Results may differ from the reference program's by a relative error of at most 0.015.
Values may be sent and summed in bfloat16 or wider, within the bound.
A program may use at most 128 MiB of HBM per device.

```python
import math
import jax
import jax.numpy as jnp
from jax import lax

B = 2
H = 48
W = 48
C = 3072
F = 12288
IMAGE_ROWS = 96
N_COL = 8


def draw_activations(key, part):
    first_key, second_key = jax.random.split(jax.random.fold_in(key, 17), 2)
    position = jnp.arange(C, dtype=jnp.float32) / C
    channel_ramp = 0.6 + 1.2 * position
    roughness = jnp.exp(jax.random.uniform(second_key, (C,), jnp.float32, -1.15, 1.15))
    values = jnp.clip(jax.random.normal(first_key, (B * H, W, C), jnp.float32), -5.0, 5.0)
    return (values * channel_ramp * roughness).astype(jnp.bfloat16)


def draw_w_expand(key, part):
    noise_key, order_key, common_key = jax.random.split(jax.random.fold_in(key, 29), 3)
    groups = N_COL
    order = jax.random.permutation(order_key, groups)
    chan_block = jnp.arange(C, dtype=jnp.int32) // (C // groups)
    unit_block = jnp.arange(F, dtype=jnp.int32) // (F // groups)
    paired = jnp.sum((unit_block[:, None] == jnp.arange(groups, dtype=jnp.int32)[None, :]).astype(jnp.int32) * order[None, :].astype(jnp.int32), 1)
    spiked = paired[None, :] == chan_block[:, None]
    factor = jnp.where(spiked, 3.0, 1.0).astype(jnp.float32)
    shared = jnp.clip(jax.random.normal(common_key, (F,), jnp.float32), -4.0, 4.0)
    noise = jnp.clip(jax.random.normal(noise_key, (C, F), jnp.float32), -6.0, 6.0)
    strength = 0.6
    values = (noise * factor + strength * shared[None, :]) / jnp.sqrt(jnp.float32(C))
    values = jnp.clip(values, -0.5, 0.5)
    return values.astype(jnp.bfloat16)


def strengthened(values, own_key, source, target, parts, factor):
    owner, partner = [(jnp.arange(values.shape[axis_at]) // (values.shape[axis_at] // parts)).reshape([-1 if axis == axis_at else 1 for axis in range(values.ndim)]) for axis_at in (source, target)]
    chosen = jax.random.permutation(own_key, parts)[partner]
    strong = (owner == chosen) | (owner == (partner + parts // 2) % parts)
    return jnp.where(strong, factor * values, values)


def block_levels(key, shape, cuts, least, top_value):
    factor_of = 1.0
    for dim, shards_of in cuts:
        steps = jax.random.uniform(jax.random.fold_in(jax.random.fold_in(key, 6), dim), (shards_of,), jnp.float32, least / len(cuts), top_value / len(cuts))
        factor_of = factor_of * jnp.repeat(jnp.exp(steps), shape[dim] // shards_of).reshape((-1,) + (1,) * (len(shape) - 1 - dim))
    return factor_of


def centred(stream_key, dims, deviation, reach, cuts=(), kind=jnp.bfloat16):
    array = deviation * jax.random.normal(stream_key, dims, jnp.float32)
    if cuts:
        array = array * block_levels(stream_key, dims, cuts, -0.22, 0.18)
    return jnp.clip(array, -reach, reach).astype(kind)


def bell_draw_with(rng, extent, spread, most, cuts, heavy, held_as=jnp.bfloat16):
    array = spread * jax.random.normal(rng, extent, jnp.float32)
    if cuts:
        array = array * block_levels(rng, extent, cuts, -0.22, 0.18)
    return jnp.clip(strengthened(array, jax.random.fold_in(rng, 3), *heavy), -most, most).astype(held_as)


def setup_inputs(seed: int = 0) -> dict:
    keys = jax.random.split(jax.random.key(seed), 11)
    return {
        "activations": draw_activations(jax.random.fold_in(keys[10], 71), 0),
        "cotangent": centred(keys[1], (IMAGE_ROWS, W, C), 1.0, 6.0, ((0, 4), (2, 8))),
        "kernel": centred(keys[2], (7, 7, C), 49 ** -0.5, 0.875, ((2, 8),), jnp.float32),
        "ln_gain": jnp.clip(1.0 + 0.15 * jax.random.normal(keys[3], (C,), jnp.float32), 0.25, 1.75),
        "ln_bias": centred(keys[4], (C,), 0.5, 3.0, (), jnp.float32),
        "w_expand": draw_w_expand(jax.random.fold_in(keys[10], 71), 0),
        "b_expand": centred(keys[6], (F,), 0.5, 3.0, ((0, 8),), jnp.float32),
        "w_reduce": bell_draw_with(keys[7], (F, C), F ** -0.5, 0.078125, ((0, 8), (1, 4)), (0, 1, 8, 2.0)),
        "b_reduce": centred(keys[8], (C,), 0.5, 3.0, ((0, 8),), jnp.float32),
        "layer_scale": jnp.clip(jnp.exp(math.log(1.5) - 1.60943787 * jax.random.uniform(keys[9], (C,), jnp.float32) ** block_levels(keys[9], (C,), ((0, 8),), -0.2, 0.2)), 0.3, 1.5),
    }


epsilon = 1e-06
root_half = 0.7071067811865476
density_scale = 0.3989422804014327

def spatial_mix(padded, weights, first_row, height):
    row_count = padded.shape[0] - 6
    col_count = padded.shape[1] - 6
    out_rows = first_row + jnp.arange(row_count, dtype=jnp.int32)
    running = jnp.zeros((row_count, col_count, padded.shape[2]), jnp.float32)
    for row_off in range(7):
        source = out_rows + (row_off - 3)
        inside = source // height == out_rows // height
        band = jnp.zeros_like(running)
        for col_off in range(7):
            band = band + weights[row_off, col_off] * padded[row_off:row_off + row_count, col_off:col_off + col_count]
        running = running + jnp.where(inside[:, None, None], band, jnp.zeros_like(band))
    return running

def gelu_slope(preact):
    cumulative = 0.5 * (1.0 + jax.scipy.special.erf(preact * root_half))
    return cumulative + preact * jnp.exp(-0.5 * preact * preact) * density_scale

def reference(activations, cotangent, kernel, ln_gain, ln_bias, w_expand, b_expand, w_reduce, b_reduce, layer_scale):
    row_total, grid_width, channels = activations.shape
    tokens = row_total * grid_width
    kernel_f = kernel.astype(jnp.float32)
    padded = jnp.pad(activations, ((3, 3), (3, 3), (0, 0))).astype(jnp.float32)
    mixed_bf = spatial_mix(padded, kernel_f, jnp.int32(0), H).astype(jnp.bfloat16)
    mixed_f = lax.optimization_barrier(mixed_bf).astype(jnp.float32).reshape(tokens, channels)
    row_mean = lax.optimization_barrier(jnp.sum(mixed_f, 1, keepdims=True)) / channels
    square = lax.optimization_barrier(jnp.sum(mixed_f * mixed_f, 1, keepdims=True)) / channels
    inv_std = lax.rsqrt(square - row_mean * row_mean + epsilon)
    normal = (mixed_f - row_mean) * inv_std
    normed = (normal * ln_gain + ln_bias).astype(jnp.bfloat16)
    preact = jnp.dot(normed, w_expand, preferred_element_type=jnp.float32) + b_expand
    hidden = jax.nn.gelu(preact, approximate=False).astype(jnp.bfloat16)
    branch_out = jnp.dot(hidden, w_reduce, preferred_element_type=jnp.float32) + b_reduce
    act_f = activations.astype(jnp.float32)
    block_out = (act_f + layer_scale * branch_out.reshape(row_total, grid_width, channels)).astype(jnp.bfloat16)
    cot_f = cotangent.astype(jnp.float32)
    grad_branch = (layer_scale * cot_f).reshape(tokens, channels).astype(jnp.bfloat16)
    grad_hidden = jnp.dot(grad_branch, w_reduce.T, preferred_element_type=jnp.float32)
    grad_preact = (grad_hidden * gelu_slope(preact)).astype(jnp.bfloat16)
    grad_normed = jnp.dot(grad_preact, w_expand.T, preferred_element_type=jnp.float32)
    grad_gain = grad_normed * ln_gain
    grad_total = lax.optimization_barrier(jnp.sum(grad_gain, 1, keepdims=True))
    grad_cross = lax.optimization_barrier(jnp.sum(grad_gain * normal, 1, keepdims=True))
    grad_mixed = inv_std * (grad_gain - grad_total / channels - normal * grad_cross / channels)
    grad_mixed = grad_mixed.astype(jnp.bfloat16).reshape(row_total, grid_width, channels)
    grad_padded = jnp.pad(grad_mixed, ((3, 3), (3, 3), (0, 0))).astype(jnp.float32)
    grad_spatial = spatial_mix(grad_padded, kernel_f[::-1, ::-1], jnp.int32(0), H).astype(jnp.bfloat16)
    grad_input = (cot_f + lax.optimization_barrier(grad_spatial).astype(jnp.float32)).astype(jnp.bfloat16)
    return (block_out, grad_input)
```

```python
import functools

import jax
import jax.numpy as jnp
from jax import lax
from jax.experimental import pallas as pl
from jax.experimental.pallas import tpu as pltpu
from jax.sharding import PartitionSpec as P

H = 48
LANES = 128

epsilon = 1e-06
root_half = 0.7071067811865476
density_scale = 0.3989422804014327


def conv_kernel(flip, add, x_ref, top_ref, bottom_ref, k_ref, *rest):
    if add:
        add_ref, o_ref, field = rest
    else:
        o_ref, field = rest
    rows, width, lanes = x_ref.shape
    field[...] = jnp.zeros_like(field)
    field[0:3, 8 : 8 + width, :] = top_ref[...].astype(jnp.float32)
    field[3 : 3 + rows, 8 : 8 + width, :] = x_ref[...].astype(jnp.float32)
    field[3 + rows : 6 + rows, 8 : 8 + width, :] = bottom_ref[...].astype(jnp.float32)

    @pl.loop(0, rows)
    def _(r):
        total = jnp.zeros((width, lanes), jnp.float32)
        for a in range(7):
            for b in range(7):
                weight = k_ref[6 - a, 6 - b] if flip else k_ref[a, b]
                total += weight[None, :] * field[r + a, 5 + b : 5 + b + width, :]
        mixed = total.astype(jnp.bfloat16)
        if add:
            mixed = (add_ref[r].astype(jnp.float32) + mixed.astype(jnp.float32)).astype(
                jnp.bfloat16
            )
        o_ref[r] = mixed


def depthwise(field, top, bottom, kernel, flip, add=None):
    rows, width, channels = field.shape
    lanes = LANES if channels % LANES == 0 else channels
    block = lambda n: pl.BlockSpec((n, width, lanes), lambda i: (0, 0, i))
    operands = [field, top, bottom, kernel]
    specs = [block(rows), block(3), block(3), pl.BlockSpec((7, 7, lanes), lambda i: (0, 0, i))]
    if add is not None:
        operands.append(add)
        specs.append(block(rows))
    return pl.pallas_call(
        functools.partial(conv_kernel, flip, add is not None),
        out_shape=jax.ShapeDtypeStruct(field.shape, jnp.bfloat16),
        grid=(channels // lanes,),
        in_specs=specs,
        out_specs=block(rows),
        scratch_shapes=[pltpu.VMEM((rows + 6, width + 16, lanes), jnp.float32)],
        compiler_params=pltpu.CompilerParams(vmem_limit_bytes=32 * 2**20),
        cost_estimate=pl.CostEstimate(
            flops=98 * rows * width * channels,
            bytes_accessed=6 * rows * width * channels,
            transcendentals=0,
        ),
        name="depthwise_flipped" if flip else "depthwise",
    )(*operands)


def halo(field):
    rows = field.shape[0]
    per_image = H // rows
    count = lax.axis_size("row")
    down = [(i, i + 1) for i in range(count - 1) if (i + 1) % per_image]
    up = [(j, i) for i, j in down]
    return lax.ppermute(field[-3:], "row", down), lax.ppermute(field[:3], "row", up)


MATMUL_VMEM = 56 * 2**20


def exchange(value, row_distance=0, masks=(0, 0), parity=0):
    rows, cols = lax.axis_size("row"), lax.axis_size("col")
    pairs = []
    for r in range(rows):
        mask = masks[0] if r % 2 == parity else masks[1]
        for c in range(cols):
            pairs.append((r * cols + c, (r ^ row_distance) * cols + (c ^ mask)))
    return lax.ppermute(value, ("row", "col"), pairs)


def orders():
    count = lax.axis_size("col")
    bits = [1 << b for b in range(1, count.bit_length() - 1)]
    half = len(bits) // 2
    return bits, bits[half:] + bits[:half]


def gather_pieces(piece, parity):
    first, second = orders()
    held = [(piece, 0, 0)]
    for one, two in zip(first, second):
        held += [
            (exchange(value, 0, (one, two), parity), a ^ one, b ^ two) for value, a, b in held
        ]
    held += [(exchange(value, 0, (1, 1)), a ^ 1, b ^ 1) for value, a, b in held]
    mine = lax.axis_index("row") % 2 == parity
    me = lax.axis_index("col")
    owners = [me ^ jnp.where(mine, a, b) for _, a, b in held]
    return [value for value, _, _ in held], jnp.stack(owners).astype(jnp.int32)


def reduce_pieces(part, parity):
    first, second = orders()
    mine = lax.axis_index("row") % 2 == parity
    me = lax.axis_index("col")
    offsets = [(0, 0)]
    for one, two in zip(first, second):
        offsets += [(a ^ one, b ^ two) for a, b in offsets]
    order = list(reversed(offsets))
    owner = lambda pair: me ^ jnp.where(mine, pair[0], pair[1])
    arrived = [
        exchange(part(owner(pair) ^ 1).astype(jnp.bfloat16), 0, (1, 1)) for pair in order
    ]
    sums = [part(owner(pair)) + got.astype(jnp.float32) for pair, got in zip(order, arrived)]
    sums.reverse()
    for one, two in reversed(list(zip(first, second))):
        half = len(sums) // 2
        moved = [
            exchange(value.astype(jnp.bfloat16), 0, (one, two), parity) for value in sums[half:]
        ]
        sums = [keep + got.astype(jnp.float32) for keep, got in zip(sums[:half], moved)]
    return sums[0]


def expand_kernel(count, channels, owners, *refs):
    pieces = refs[:count]
    weights, bias, gain, shift, hidden, slope, preact_out, mean_out, inv_out = refs[count:]
    total = square = 0.0
    for ref in pieces:
        value = ref[...].astype(jnp.float32)
        total += jnp.sum(value, 1, keepdims=True)
        square += jnp.sum(value * value, 1, keepdims=True)
    mean = total / channels
    inv = lax.rsqrt(square / channels - mean * mean + epsilon)
    preact = bias[...]
    for index, ref in enumerate(pieces):
        owner = owners[index]
        normal = (ref[...].astype(jnp.float32) - mean) * inv
        normed = (normal * gain[owner] + shift[owner]).astype(jnp.bfloat16)
        preact = preact + jnp.dot(normed, weights[owner], preferred_element_type=jnp.float32)
    cumulative = 0.5 * (1.0 + lax.erf(preact * root_half))
    hidden[...] = (preact * cumulative).astype(jnp.bfloat16)
    slope[...] = cumulative + preact * jnp.exp(-0.5 * preact * preact) * density_scale
    preact_out[...] = preact
    mean_out[...] = mean
    inv_out[...] = inv


def token_tile(tokens):
    for tile in (384, 288, 192, 96, 64, 48, 32, 16):
        if tokens % tile == 0:
            return tile
    return tokens


def expand(pieces, owners, weights, bias, gain, shift, channels):
    tokens, narrow = pieces[0].shape
    count, _, units = weights.shape
    tile = token_tile(tokens)
    row = lambda width: pl.BlockSpec((tile, width), lambda i, *_: (i, 0))
    whole = lambda array: pl.BlockSpec(array.shape, lambda i, *_: (0,) * array.ndim)
    operands = [weights, bias[None, :], gain.reshape(count, 1, narrow), shift.reshape(count, 1, narrow)]
    wide = jax.ShapeDtypeStruct((tokens, units), jnp.float32)
    thin = jax.ShapeDtypeStruct((tokens, 1), jnp.float32)
    return pl.pallas_call(
        functools.partial(expand_kernel, count, channels),
        grid_spec=pltpu.PrefetchScalarGridSpec(
            num_scalar_prefetch=1,
            grid=(tokens // tile,),
            in_specs=[row(narrow)] * count + [whole(array) for array in operands],
            out_specs=[row(units), row(units), row(units), row(1), row(1)],
        ),
        out_shape=[jax.ShapeDtypeStruct((tokens, units), jnp.bfloat16), wide, wide, thin, thin],
        compiler_params=pltpu.CompilerParams(vmem_limit_bytes=MATMUL_VMEM),
        cost_estimate=pl.CostEstimate(
            flops=2 * tokens * channels * units,
            bytes_accessed=2 * tokens * channels + 2 * channels * units + 10 * tokens * units,
            transcendentals=2 * tokens * units,
        ),
        name="expand",
    )(owners, *pieces, *operands)


def slope_kernel(count, owners, *refs):
    pieces = refs[:count]
    weights, slope, preact, known, vector, out, sums = refs[count:]
    grad_hidden = 0.0
    for index, ref in enumerate(pieces):
        grad_hidden += lax.dot_general(
            ref[...],
            weights[owners[index]],
            (((1,), (1,)), ((), ())),
            preferred_element_type=jnp.float32,
        )
    grad = (grad_hidden * slope[...]).astype(jnp.bfloat16)
    out[...] = grad
    grad = grad.astype(jnp.float32)
    total = jnp.sum(grad * vector[...], 1, keepdims=True)
    cross = jnp.sum(grad * (preact[...] - known[...]), 1, keepdims=True)
    sums[...] = jnp.concatenate([total, cross], 1)


def grad_units(pieces, owners, weights, slope, preact, known, vector):
    tokens, narrow = pieces[0].shape
    count, units, _ = weights.shape
    tile = token_tile(tokens)
    row = lambda width: pl.BlockSpec((tile, width), lambda i, *_: (i, 0))
    whole = lambda array: pl.BlockSpec(array.shape, lambda i, *_: (0,) * array.ndim)
    return pl.pallas_call(
        functools.partial(slope_kernel, count),
        grid_spec=pltpu.PrefetchScalarGridSpec(
            num_scalar_prefetch=1,
            grid=(tokens // tile,),
            in_specs=[row(narrow)] * count
            + [whole(weights), row(units), row(units)]
            + [pl.BlockSpec((1, units), lambda i, *_: (0, 0))] * 2,
            out_specs=[row(units), row(2)],
        ),
        out_shape=[
            jax.ShapeDtypeStruct((tokens, units), jnp.bfloat16),
            jax.ShapeDtypeStruct((tokens, 2), jnp.float32),
        ],
        compiler_params=pltpu.CompilerParams(vmem_limit_bytes=MATMUL_VMEM),
        cost_estimate=pl.CostEstimate(
            flops=2 * tokens * count * narrow * units,
            bytes_accessed=2 * (tokens + units) * count * narrow + 10 * tokens * units,
            transcendentals=0,
        ),
        name="grad_units",
    )(owners, *pieces, weights, slope, preact, known[None, :], vector[None, :])


def body(
    activations,
    cotangent,
    kernel,
    ln_gain,
    ln_bias,
    w_expand,
    b_expand,
    w_reduce,
    b_reduce,
    layer_scale,
):
    row_count, grid_width, narrow = activations.shape
    rows, cols = lax.axis_size("row"), lax.axis_size("col")
    me_row, me_col = lax.axis_index("row"), lax.axis_index("col")
    channels = narrow * cols
    depth = channels // rows
    tokens = row_count * grid_width
    units = w_expand.shape[1] // 2
    parity = me_row % 2

    top, bottom = halo(activations)
    cot_f = cotangent.astype(jnp.float32)
    grad_branch = (layer_scale * cot_f).reshape(tokens, narrow).astype(jnp.bfloat16)

    expand_halves = [
        lax.dynamic_slice_in_dim(w_expand, (parity ^ flip) * units, units, 1) for flip in (0, 1)
    ]
    slabs = w_reduce.reshape(2, units, depth // narrow, narrow).transpose(0, 2, 1, 3)
    reduce_halves = [
        lax.dynamic_index_in_dim(slabs, parity ^ flip, 0, keepdims=False) for flip in (0, 1)
    ]

    def assemble(halves, sent):
        own = halves[0]
        out = jnp.zeros((rows,) + own.shape, own.dtype)
        for distance in range(rows):
            block = sent[distance] if distance else own
            out = lax.dynamic_update_index_in_dim(out, block, me_row ^ distance, 0)
        return out

    expand_sent = [None] + [exchange(expand_halves[d % 2], d) for d in range(1, rows)]
    grad_partner = exchange(grad_branch, 1)
    grad_own_pieces, own_owners = gather_pieces(grad_branch, 0)
    grad_partner_pieces, partner_owners = gather_pieces(grad_partner, 1)

    mixed = depthwise(activations, top, bottom, kernel, False).reshape(tokens, narrow)
    mixed_partner = exchange(mixed, 1)
    mixed_own_pieces, _ = gather_pieces(mixed, 0)
    mixed_partner_pieces, _ = gather_pieces(mixed_partner, 1)

    held = lax.optimization_barrier((*reduce_halves, *expand_sent[1:]))
    reduce_halves, expand_sent = held[:2], (None,) + tuple(held[2:])
    reduce_sent = [None] + [exchange(reduce_halves[d % 2], d) for d in range(1, rows)]

    expand_full = assemble(expand_halves, expand_sent).reshape(cols, narrow, units)
    bias = lax.dynamic_slice_in_dim(b_expand, parity * units, units)
    own = expand(mixed_own_pieces, own_owners, expand_full, bias, ln_gain, ln_bias, channels)
    other = expand(
        mixed_partner_pieces, partner_owners, expand_full, bias, ln_gain, ln_bias, channels
    )
    mean, inv_std = own[3], own[4]
    vectors = jnp.stack([ln_gain, ln_bias])
    gain_unit, bias_unit = jnp.dot(
        vectors,
        expand_full.reshape(channels, units).astype(jnp.float32),
        precision=lax.Precision.HIGHEST,
    )

    reduce_full = assemble(reduce_halves, reduce_sent).reshape(cols, units, narrow)
    known = bias + bias_unit
    grad_own, sums_own = grad_units(
        grad_own_pieces, own_owners, reduce_full, own[1], own[2], known, gain_unit
    )
    grad_other, sums_other = grad_units(
        grad_partner_pieces, partner_owners, reduce_full, other[1], other[2], known, gain_unit
    )

    def branch_part(hidden):
        return lambda owner: jnp.dot(
            hidden,
            lax.dynamic_index_in_dim(reduce_full, owner, 0, keepdims=False),
            preferred_element_type=jnp.float32,
        )

    def grad_part(grad):
        return lambda owner: lax.dot_general(
            grad,
            lax.dynamic_index_in_dim(expand_full, owner, 0, keepdims=False),
            (((1,), (1,)), ((), ())),
            preferred_element_type=jnp.float32,
        )

    def pair_sum(part, own_value, other_value):
        away = reduce_pieces(part(other_value), 1).astype(jnp.bfloat16)
        return reduce_pieces(part(own_value), 0) + exchange(away, 1).astype(jnp.float32)

    branch = pair_sum(branch_part, own[0], other[0]) + b_reduce
    local_gain = lax.dynamic_slice_in_dim(ln_gain, me_col * narrow, narrow)
    grad_gain = pair_sum(grad_part, grad_own, grad_other) * local_gain

    sums = sums_own.T + exchange(sums_other.T, 1)
    distance = 1
    while distance < cols:
        sums = sums + exchange(sums, 0, (distance, distance))
        distance *= 2
    normal = (mixed.astype(jnp.float32) - mean) * inv_std
    grad_mixed = inv_std * (
        grad_gain - sums[0][:, None] / channels - normal * sums[1][:, None] / channels
    )
    grad_mixed = grad_mixed.astype(jnp.bfloat16).reshape(row_count, grid_width, narrow)
    top, bottom = halo(grad_mixed)
    grad_input = depthwise(grad_mixed, top, bottom, kernel, True, cotangent)

    act_f = activations.astype(jnp.float32)
    block_out = (act_f + layer_scale * branch.reshape(row_count, grid_width, narrow)).astype(
        jnp.bfloat16
    )
    return (block_out, grad_input)


def solution(mesh):
    return jax.shard_map(
        body,
        mesh=mesh,
        in_specs=(
            P("row", None, "col"),
            P("row", None, "col"),
            P(None, None, "col"),
            P(),
            P(),
            P("row", "col"),
            P("col"),
            P("col", "row"),
            P("col"),
            P("col"),
        ),
        out_specs=(P("row", None, "col"), P("row", None, "col")),
        check_vma=False,
    )
```

```python
import functools

import jax
import jax.numpy as jnp
from jax import lax
from jax.experimental import pallas as pl
from jax.experimental.pallas import tpu as pltpu
from jax.sharding import PartitionSpec as P

H = 48
LANES = 128

epsilon = 1e-06
root_half = 0.7071067811865476
density_scale = 0.3989422804014327


def conv_kernel(flip, add, x_ref, top_ref, bottom_ref, k_ref, *rest):
    if add:
        add_ref, o_ref, field = rest
    else:
        o_ref, field = rest
    rows, width, lanes = x_ref.shape
    field[...] = jnp.zeros_like(field)
    field[0:3, 8 : 8 + width, :] = top_ref[...].astype(jnp.float32)
    field[3 : 3 + rows, 8 : 8 + width, :] = x_ref[...].astype(jnp.float32)
    field[3 + rows : 6 + rows, 8 : 8 + width, :] = bottom_ref[...].astype(jnp.float32)

    @pl.loop(0, rows)
    def _(r):
        total = jnp.zeros((width, lanes), jnp.float32)
        for a in range(7):
            for b in range(7):
                weight = k_ref[6 - a, 6 - b] if flip else k_ref[a, b]
                total += weight[None, :] * field[r + a, 5 + b : 5 + b + width, :]
        mixed = total.astype(jnp.bfloat16)
        if add:
            mixed = (add_ref[r].astype(jnp.float32) + mixed.astype(jnp.float32)).astype(
                jnp.bfloat16
            )
        o_ref[r] = mixed


def depthwise(field, top, bottom, kernel, flip, add=None):
    rows, width, channels = field.shape
    lanes = LANES if channels % LANES == 0 else channels
    block = lambda n: pl.BlockSpec((n, width, lanes), lambda i: (0, 0, i))
    operands = [field, top, bottom, kernel]
    specs = [block(rows), block(3), block(3), pl.BlockSpec((7, 7, lanes), lambda i: (0, 0, i))]
    if add is not None:
        operands.append(add)
        specs.append(block(rows))
    return pl.pallas_call(
        functools.partial(conv_kernel, flip, add is not None),
        out_shape=jax.ShapeDtypeStruct(field.shape, jnp.bfloat16),
        grid=(channels // lanes,),
        in_specs=specs,
        out_specs=block(rows),
        scratch_shapes=[pltpu.VMEM((rows + 6, width + 16, lanes), jnp.float32)],
        compiler_params=pltpu.CompilerParams(vmem_limit_bytes=32 * 2**20),
        cost_estimate=pl.CostEstimate(
            flops=98 * rows * width * channels,
            bytes_accessed=6 * rows * width * channels,
            transcendentals=0,
        ),
        name="depthwise_flipped" if flip else "depthwise",
    )(*operands)


def halo(field):
    rows = field.shape[0]
    per_image = H // rows
    count = lax.axis_size("row")
    down = [(i, i + 1) for i in range(count - 1) if (i + 1) % per_image]
    up = [(j, i) for i, j in down]
    return lax.ppermute(field[-3:], "row", down), lax.ppermute(field[:3], "row", up)


MESH = pl.DeviceIdType.MESH
VMEM_LIMIT = 63 * 2**20


def flip(index, bit):
    return index + bit - 2 * bit * ((index // bit) % 2)


def flip_all(index, mask):
    bit = 1
    while bit <= mask:
        if mask & bit:
            index = flip(index, bit)
        bit *= 2
    return index


def token_tile(tokens):
    for tile in (384, 192, 96, 48, 16):
        if tokens % tile == 0:
            return tile
    return tokens


def split_columns(narrow, first):
    if narrow % LANES:
        return [(0, narrow)]
    groups = narrow // LANES
    head = min(first, groups)
    ranges = [(0, head * LANES)]
    if groups > head:
        ranges.append((head * LANES, (groups - head) * LANES))
    return ranges


def block_kernel(
    rows,
    cols,
    act,
    grad,
    w_expand,
    w_reduce,
    taps,
    bias,
    gain,
    shift,
    vectors,
    local_gain,
    scale,
    b_reduce,
    out,
    grad_mixed,
    mixes,
    grads,
    stage,
    expand,
    reduce,
    hidden,
    slopes,
    preact,
    mixed,
    stats,
    units_in,
    sums,
    sums_in,
    top,
    bottom,
    send,
    recv,
    local,
    free,
):
    tokens, narrow = grad.shape
    row_count, width, _ = act.shape
    channels = narrow * cols
    depth, units = expand.shape[1:]
    per = depth // narrow
    sliced = narrow % LANES == 0
    tile = token_tile(tokens)
    tiles = tokens // tile
    per_image = H // row_count
    r, c = lax.axis_index("row"), lax.axis_index("col")
    parity = r % 2
    blocks = cols // 2
    bits = [1 << b for b in range(1, cols.bit_length() - 1)]
    steps = len(bits)
    second = bits[steps // 2 :] + bits[: steps // 2]
    f32, bf16 = jnp.float32, jnp.bfloat16
    dot = functools.partial(jnp.dot, preferred_element_type=f32)
    turned = lambda left, right: lax.dot_general(
        left, right, (((1,), (1,)), ((), ())), preferred_element_type=f32
    )
    row_of = lambda distance: (flip_all(r, distance), c)
    core = (r, flip(c, 1))
    partner = row_of(1)

    def step_column(index, half, s):
        e = (r + half) % 2
        return flip(index, bits[s]) * (1 - e) + flip(index, second[s]) * e

    def owner_of(half, j):
        index = c
        for s in range(steps):
            index = index + ((j // (1 << s)) % 2) * (step_column(index, half, s) - index)
        return index

    counter = [0]

    def new(count=1):
        counter[0] += count
        return counter[0] - count

    def remote(src, dst, sem, device):
        return pltpu.make_async_remote_copy(
            src_ref=src,
            dst_ref=dst,
            send_sem=send.at[sem],
            recv_sem=recv.at[sem],
            device_id=device,
            device_id_type=MESH,
        )

    barrier = pltpu.get_barrier_semaphore()
    others = [row_of(d) for d in range(1, rows)] + [(r, flip(c, bit)) for bit in [1] + bits]
    for device in others:
        pl.semaphore_signal(barrier, inc=1, device_id=device, device_id_type=MESH)
    pl.semaphore_wait(barrier, len(others))

    has_top, has_bottom = r % per_image != 0, (r + 1) % per_image != 0
    up_device = ((r + rows - 1) % rows, c)
    down_device = ((r + 1) % rows, c)
    down = remote(act.at[pl.ds(row_count - 3, 3)], top, new(), down_device)
    up = remote(act.at[pl.ds(0, 3)], bottom, new(), up_device)
    if per_image > 1:
        pl.when(has_bottom)(down.start)
        pl.when(has_top)(up.start)

    def parts_of_expand(distance):
        half = (flip_all(r, distance) % 2) * units
        return w_expand.at[:, pl.ds(pl.multiple_of(half, units), units)]

    reduce_ranges = split_columns(narrow, 2)

    def parts_of_reduce(distance, start, size):
        half = flip_all(r, distance) % 2
        pairs = []
        for i in range(per):
            if sliced:
                span = pl.ds(i * narrow + start, size)
                rows_of = pl.ds(pl.multiple_of(half * units, units), units)
                pairs.append((w_reduce.at[rows_of, span], reduce.at[r, :, span]))
            else:
                pairs.append((w_reduce.at[half, i], reduce.at[r * per + i]))
        return pairs

    def loads(pairs, base):
        copies = []
        for index, (src, dst) in enumerate(pairs):
            copies.append(pltpu.make_async_copy(src, dst, local.at[base + index]))
            copies[-1].start()
        return copies

    taken = stage.at[0]
    act_in = [
        pltpu.make_async_copy(
            act.at[i], taken.at[pl.ds(i * width, width)], local.at[0]
        )
        for i in range(row_count)
    ]
    expand_own = loads([(parts_of_expand(0), expand.at[r])], 3)
    grad_own = loads([(grad, grads.at[0, c])], 4)

    expand_copies = [
        remote(parts_of_expand(d), expand.at[r], new(), row_of(d)) for d in range(rows - 1, 0, -1)
    ]

    def gather(buffer, source):
        step_copies = [[], []]
        for half in (0, 1):
            for s in range(steps):
                step_copies[half].append(
                    [
                        remote(
                            source if half == 0 and j == 0 else buffer.at[half, owner_of(half, j)],
                            buffer.at[half, owner_of(half, j)],
                            new(),
                            (r, step_column(c, half, s)),
                        )
                        for j in range(1 << s)
                    ]
                )
        across = remote(source, buffer.at[1, c], new(), partner)
        core_copies = [
            [
                remote(
                    source if half == 0 and j == 0 else buffer.at[half, owner_of(half, j)],
                    buffer.at[half, owner_of(half, j)],
                    new(),
                    core,
                )
                for j in range(blocks)
            ]
            for half in (0, 1)
        ]
        return step_copies, across, core_copies

    grad_steps, grad_across, grad_core = gather(grads, grad)
    mix_steps, mix_across, mix_core = gather(mixes, mixed)

    def begin(copies):
        for copy in copies:
            copy.start()

    def arrive(copies):
        for copy in copies:
            copy.wait_recv()

    def leave(copies):
        for copy in copies:
            copy.wait_send()

    begin(grad_steps[0][0])
    begin(expand_copies[:1])
    reduce_own = loads(
        [pair for start, size in reduce_ranges for pair in parts_of_reduce(0, start, size)], 5
    )

    for i in range(row_count):
        act_in[i].start()
        act_in[i].wait()
    if per_image > 1:

        @pl.when(has_top)
        def _():
            down.wait_recv()

        @pl.when(has_bottom)
        def _():
            up.wait_recv()

    lanes = LANES if sliced else narrow
    pitch = preact.shape[1]

    def place(row, value):
        preact[row, 8 : 8 + width, 0:lanes] = value.astype(f32)

    for group in range(narrow // lanes):
        span = pl.ds(group * lanes, lanes)

        @pl.loop(0, row_count + 6)
        def _(i):
            preact[i, :, 0:lanes] = jnp.zeros((pitch, lanes), f32)

        @pl.loop(0, row_count)
        def _(i):
            place(i + 3, stage[0, pl.ds(pl.multiple_of(i * width, 16), width), span])

        if per_image > 1:

            @pl.when(has_top)
            def _():
                for i in range(3):
                    place(i, top[i, :, span])

            @pl.when(has_bottom)
            def _():
                for i in range(3):
                    place(i + row_count + 3, bottom[i, :, span])

        @pl.loop(0, row_count)
        def _(i):
            total = jnp.zeros((width, lanes), f32)
            for a in range(7):
                for b in range(7):
                    total += (
                        taps[a, b, span][None, :]
                        * preact[i + a, 5 + b : 5 + b + width, 0:lanes]
                    )
            value = total.astype(bf16)
            mixed[pl.ds(pl.multiple_of(i * width, 16), width), span] = value

    begin([mix_across])
    begin(mix_steps[0][0])
    own_mixed = loads([(mixed, mixes.at[0, c])], 1)
    begin(mix_core[0][:1])
    begin([grad_across])
    begin(expand_copies[1:])
    for copy in own_mixed + grad_own:
        copy.wait()
    arrive([mix_across])
    begin(mix_steps[1][0])
    begin(mix_core[1][:1])
    for s in range(steps):
        for half in (0, 1):
            arrive(mix_steps[half][s])
            if s + 1 < steps:
                begin(mix_steps[half][s + 1])
            begin(mix_core[half][1 << s : 2 << s])
        if s == 0:
            arrive(grad_steps[0][0])
            if steps > 1:
                begin(grad_steps[0][1])
            arrive([grad_across])
            begin(grad_steps[1][0])
            begin(grad_core[0][:1] + grad_core[1][:1])
    arrive(grad_steps[1][0])
    if steps > 1:
        begin(grad_steps[1][1])
    for half in (0, 1):
        begin(grad_core[half][1:2])

    for copy in expand_own:
        copy.wait()
    arrive(expand_copies)
    for copy in reduce_own:
        copy.wait()
    reduce_copies = []
    for start, size in reduce_ranges:
        copies = []
        for d in range(rows - 1, 0, -1):
            copies += [
                remote(src, dst, new(), row_of(d)) for src, dst in parts_of_reduce(d, start, size)
            ]
        reduce_copies.append(copies)
    begin(reduce_copies[0])

    extra = jnp.zeros((vectors.shape[1], units), f32)
    for b in range(rows):
        extra += dot(vectors[b], expand[b])
    units_in[0:1, :] = extra[0:1] + extra[1:2] + extra[2:3]
    units_in[1:2, :] = bias[...] + (extra[3:4] + extra[4:5] + extra[5:6])

    def at(half, t):
        return pl.ds(pl.multiple_of(half * tokens + t * tile, 16), tile)

    def group_at(half, t):
        return pl.ds(half * (tokens // pitch) + t * (tile // pitch), tile // pitch)

    def expand_tokens(half):
        @pl.loop(0, tiles)
        def _(t):
            rows_at = pl.ds(pl.multiple_of(t * tile, 16), tile)
            total = jnp.zeros((tile, 1), f32)
            square = jnp.zeros((tile, 1), f32)
            for o in range(cols):
                value = mixes[half, o, rows_at, :].astype(f32)
                total += jnp.sum(value, 1, keepdims=True)
                square += jnp.sum(value * value, 1, keepdims=True)
            mean = total / channels
            inv = lax.rsqrt(square / channels - mean * mean + epsilon)
            if half == 0:
                stats[rows_at, 0:1] = mean
                stats[rows_at, 1:2] = inv
            value = jnp.zeros((tile, units), f32) + bias[...]
            for b in range(rows):
                group = [b * per + i for i in range(per)]
                normed = [
                    (
                        (mixes[half, o, rows_at, :].astype(f32) - mean) * inv * gain[o] + shift[o]
                    ).astype(bf16)
                    for o in group
                ]
                if sliced:
                    value += dot(jnp.concatenate(normed, 1), expand[b])
                else:
                    for i in range(per):
                        value += dot(normed[i], expand[b, i * narrow : (i + 1) * narrow, :])
            cumulative = 0.5 * (1.0 + lax.erf(value * root_half))
            hidden[at(half, t), :] = (value * cumulative).astype(bf16)
            preact[group_at(half, t)] = value.reshape(-1, pitch, units)

    arrive(mix_core[0])
    expand_tokens(0)
    for half in (0, 1):
        for s in range(1, steps):
            arrive(grad_steps[half][s])
            if s + 1 < steps:
                begin(grad_steps[half][s + 1])
            begin(grad_core[half][1 << s : 2 << s])
    arrive(mix_core[1])
    expand_tokens(1)

    nearby = [core, partner] + [(r, flip(c, bit)) for bit in bits]

    def release(index):
        for device in nearby:
            pl.semaphore_signal(free.at[index], inc=1, device_id=device, device_id_type=MESH)

    for half in (0, 1):
        for s in range(steps):
            leave(mix_steps[half][s])
        leave(mix_core[half])
    leave([mix_across])
    release(0)

    def sum_part(buffer, part, start, size, emit):
        base = new(4 * blocks - 1)
        span = pl.ds(start, size)

        def core_copy(half, j, slot):
            return remote(
                stage.at[slot, :, span], buffer.at[half, j, :, span], base + half * blocks + j, core
            )

        def step_copy(half, s, i):
            return remote(
                stage.at[2 * ((1 << s) - 1) + 2 * i + half, :, span],
                buffer.at[half, blocks + (1 << s) - 1 + i, :, span],
                base + 2 * blocks + 2 * ((1 << s) - 1) + 2 * i + half,
                (r, step_column(c, half, s)),
            )

        pair_copy = remote(
            stage.at[2 * (blocks - 1), :, span],
            buffer.at[0, cols - 1, :, span],
            base + 4 * blocks - 2,
            partner,
        )

        def total(half, t, owner, j, later):
            rows_at = pl.ds(pl.multiple_of(t * tile, 16), tile)
            value = part(half, t, owner, start, size)
            value += buffer[half, j, rows_at, span].astype(f32)
            for s in later:
                value += buffer[half, blocks + (1 << s) - 1 + j, rows_at, span].astype(f32)
            return value

        def over_tiles(slot, value_of):
            @pl.loop(0, tiles)
            def _(t):
                rows_at = pl.ds(pl.multiple_of(t * tile, 16), tile)
                stage[slot, rows_at, span] = value_of(t).astype(bf16)

        def first():
            @pl.loop(0, 2 * blocks)
            def _(i):
                half, j = i % 2, blocks - 1 - i // 2
                owner = flip(owner_of(half, j), 1)
                over_tiles(i, lambda t: part(half, t, owner, start, size))
                core_copy(half, j, i).start()

        def clear():
            @pl.loop(0, 2 * blocks)
            def _(i):
                core_copy(i % 2, blocks - 1 - i // 2, i).wait_send()

        def step(s):
            @pl.loop(0, 2 << s)
            def _(n):
                half, i = n % 2, n // 2
                j = i + (1 << s)
                core_copy(half, j, 0).wait_recv()
                for later in range(s + 1, steps):
                    step_copy(half, later, j).wait_recv()
                owner = owner_of(half, j)
                over_tiles(
                    2 * ((1 << s) - 1) + n,
                    lambda t: total(half, t, owner, j, range(s + 1, steps)),
                )
                step_copy(half, s, i).start()

        def across():
            core_copy(1, 0, 0).wait_recv()
            for s in range(steps):
                step_copy(1, s, 0).wait_recv()
            over_tiles(2 * (blocks - 1), lambda t: total(1, t, c, 0, range(steps)))
            pair_copy.start()

        def last():
            core_copy(0, 0, 0).wait_recv()
            for s in range(steps):
                step_copy(0, s, 0).wait_recv()
            pair_copy.wait_recv()

            @pl.loop(0, tiles)
            def _(t):
                rows_at = pl.ds(pl.multiple_of(t * tile, 16), tile)
                value = total(0, t, c, 0, range(steps))
                value += buffer[0, cols - 1, rows_at, span].astype(f32)
                emit(t, rows_at, span, start, size, value)

        def finish():
            for s in range(steps):

                @pl.loop(0, 2 << s)
                def _(n):
                    step_copy(n % 2, s, n // 2).wait_send()

            pair_copy.wait_send()

        stages = [first, clear] + [functools.partial(step, s) for s in range(steps - 1, -1, -1)]
        return stages + [across, last, finish]

    def branch_part(half, t, owner, start, size):
        if sliced:
            at_lane = pl.multiple_of((owner % per) * narrow + start, LANES)
            weights = reduce[owner // per, :, pl.ds(at_lane, size)]
        else:
            weights = reduce[owner]
        return dot(hidden[at(half, t), :], weights)

    def grad_part(half, t, owner, start, size):
        at_row = pl.multiple_of((owner % per) * narrow + start, 16)
        return turned(slopes[at(half, t), :], expand[owner // per, pl.ds(at_row, size), :])

    def emit_branch(t, rows_at, span, start, size, value):
        lane = slice(start, start + size)
        value = scale[:, lane] * (value + b_reduce[:, lane])
        value += stage[2 * blocks - 1, rows_at, span].astype(f32)
        stage[2 * blocks - 1, rows_at, span] = value.astype(bf16)

    def emit_grad(t, rows_at, span, start, size, value):
        lane = slice(start, start + size)
        mean, inv = stats[rows_at, 0:1], stats[rows_at, 1:2]
        both = jnp.transpose(sums[0, t])
        normal = (mixed[rows_at, span].astype(f32) - mean) * inv
        value = value * local_gain[:, lane]
        value = inv * (value - both[:, 0:1] / channels - normal * both[:, 1:2] / channels)
        mixed[rows_at, span] = value.astype(bf16)

    def grad_tokens(half):
        @pl.loop(0, tiles)
        def _(t):
            rows_at = pl.ds(pl.multiple_of(t * tile, 16), tile)
            value = jnp.zeros((tile, units), f32)
            for b in range(rows):
                group = [grads[half, b * per + i, rows_at, :] for i in range(per)]
                if sliced:
                    value += turned(jnp.concatenate(group, 1), reduce[b])
                else:
                    for i in range(per):
                        value += turned(group[i], reduce[b * per + i])
            a = preact[group_at(half, t)].reshape(tile, units)
            cumulative = 0.5 * (1.0 + lax.erf(a * root_half))
            slope = cumulative + a * jnp.exp(-0.5 * a * a) * density_scale
            rounded = (value * slope).astype(bf16)
            slopes[at(half, t), :] = rounded
            rounded = rounded.astype(f32)
            total = jnp.sum(rounded * units_in[0:1, :], 1, keepdims=True)
            cross = jnp.sum(rounded * (a - units_in[1:2, :]), 1, keepdims=True)
            lane = lax.broadcasted_iota(jnp.int32, (tile, LANES), 1)
            both = jnp.where(lane == 0, total, jnp.where(lane == 1, cross, 0.0))
            sums[half, t] = jnp.transpose(both)[0:8]

    arrive(reduce_copies[0])
    for copies in reduce_copies[1:]:
        begin(copies)
    pl.semaphore_wait(free.at[0], len(nearby))
    branch_parts = [
        sum_part(mixes, branch_part, start, size, emit_branch) for start, size in reduce_ranges
    ]
    head = branch_parts[0]
    for run in head[:-3]:
        run()
    for half in (0, 1):
        arrive(grad_core[half])
    for copies in reduce_copies[1:]:
        arrive(copies)
    tail = branch_parts[1] if len(branch_parts) > 1 else None
    if tail:
        tail[0]()
        tail[1]()
    grad_tokens(0)
    head[-3]()
    if tail:
        tail[2]()
    grad_tokens(1)
    for half in (0, 1):
        for s in range(steps):
            leave(grad_steps[half][s])
        leave(grad_core[half])
    leave([grad_across])
    release(1)

    sum_devices = [partner] + [(r, flip(c, bit)) for bit in [1] + bits]
    sum_copies = [
        remote(sums.at[1 if n == 0 else 0], sums_in.at[n], new(), device)
        for n, device in enumerate(sum_devices)
    ]

    def sum_step(n):
        if n:
            sum_copies[n - 1].wait()
            sums[0] = sums[0] + sums_in[n - 1]
        if n < len(sum_copies):
            sum_copies[n].start()

    sum_step(0)
    if tail:
        for run in tail[3:-2]:
            run()
    final_act = [
        pltpu.make_async_copy(
            act.at[i],
            stage.at[2 * blocks - 1, pl.ds(i * width, width)],
            local.at[0],
        )
        for i in range(row_count)
    ]
    for copy in final_act:
        copy.start()
        copy.wait()
    for run in head[-2:]:
        run()
    if tail:
        for run in tail[-2:]:
            run()
    out_copy = pltpu.make_async_copy(stage.at[2 * blocks - 1], out, local.at[0])
    out_copy.start()
    out_copy.wait()
    pl.semaphore_wait(free.at[1], len(nearby))

    grad_parts = [
        sum_part(grads, grad_part, start, size, emit_grad) for start, size in split_columns(narrow, 2)
    ]
    sum_index = 1
    for level in range(len(grad_parts[0]) - 2):
        for stages in grad_parts:
            stages[level]()
        if sum_index <= len(sum_copies):
            sum_step(sum_index)
            sum_index += 1
    while sum_index <= len(sum_copies):
        sum_step(sum_index)
        sum_index += 1
    for stages in grad_parts:
        stages[-2]()
    grad_copy = pltpu.make_async_copy(mixed, grad_mixed, local.at[1])
    grad_copy.start()
    for stages in grad_parts:
        stages[-1]()
    grad_copy.wait()

    leave(expand_copies)
    for copies in reduce_copies:
        leave(copies)
    if per_image > 1:
        pl.when(has_bottom)(down.wait_send)
        pl.when(has_top)(up.wait_send)


def semaphores_needed(rows, cols, per, reduce_parts, grad_parts):
    blocks, steps = cols // 2, cols.bit_length() - 2
    gathers = 2 * (2 * (blocks - 1) + 1 + 2 * blocks)
    weights = (rows - 1) * (1 + per * reduce_parts)
    return 2 + weights + gathers + (reduce_parts + grad_parts) * (4 * blocks - 1) + steps + 2


def body(
    activations,
    cotangent,
    kernel,
    ln_gain,
    ln_bias,
    w_expand,
    b_expand,
    w_reduce,
    b_reduce,
    layer_scale,
):
    row_count, grid_width, narrow = activations.shape
    rows, cols = lax.axis_size("row"), lax.axis_size("col")
    me_row, me_col = lax.axis_index("row"), lax.axis_index("col")
    channels = narrow * cols
    depth = channels // rows
    per = depth // narrow
    tokens = row_count * grid_width
    units = w_expand.shape[1] // 2
    sliced = narrow % LANES == 0
    tile = token_tile(tokens)
    f32, bf16 = jnp.float32, jnp.bfloat16

    cot_f = cotangent.astype(f32)
    grad_branch = (layer_scale * cot_f).reshape(tokens, narrow).astype(bf16)
    bias = lax.dynamic_slice_in_dim(b_expand, (me_row % 2) * units, units)[None, :]
    exact = []
    for vector in (ln_gain, ln_bias):
        for _ in range(3):
            piece = lax.reduce_precision(vector, 8, 7)
            exact.append(piece.astype(bf16))
            vector = vector - piece
    exact += [jnp.zeros_like(exact[0])] * (16 - len(exact))
    vectors = jnp.stack(exact).reshape(16, rows, depth).transpose(1, 0, 2)
    if sliced:
        reduce_source = w_reduce
        reduce_shape = (rows, units, depth)
    else:
        reduce_source = w_reduce.reshape(2, units, per, narrow).transpose(0, 2, 1, 3)
        reduce_shape = (cols, units, narrow)
    local_gain = lax.dynamic_slice_in_dim(ln_gain, me_col * narrow, narrow)
    reduce_parts = len(split_columns(narrow, 2))
    count = semaphores_needed(rows, cols, per, reduce_parts, len(split_columns(narrow, 2)))
    steps = cols.bit_length() - 2

    anywhere = pl.BlockSpec(memory_space=pl.ANY)
    inside = pl.BlockSpec(memory_space=pltpu.VMEM)
    flops = 8 * 2 * tokens * channels * units
    block_out, grad_mixed = pl.pallas_call(
        functools.partial(block_kernel, rows, cols),
        out_shape=[jax.ShapeDtypeStruct((tokens, narrow), bf16)] * 2,
        in_specs=[anywhere] * 4 + [inside] * 8,
        out_specs=[anywhere] * 2,
        scratch_shapes=[
            pltpu.VMEM((2, cols, tokens, narrow), bf16),
            pltpu.VMEM((2, cols, tokens, narrow), bf16),
            pltpu.VMEM((cols, tokens, narrow), bf16),
            pltpu.VMEM((rows, depth, units), bf16),
            pltpu.VMEM(reduce_shape, bf16),
            pltpu.VMEM((2 * tokens, units), bf16),
            pltpu.VMEM((2 * tokens, units), bf16),
            pltpu.VMEM((2 * tokens // (grid_width + 16), grid_width + 16, units), f32),
            pltpu.VMEM((tokens, narrow), bf16),
            pltpu.VMEM((tokens, 2), f32),
            pltpu.VMEM((2, units), f32),
            pltpu.VMEM((2, tokens // tile, 8, tile), f32),
            pltpu.VMEM((steps + 2, tokens // tile, 8, tile), f32),
            pltpu.VMEM((3, grid_width, narrow), bf16),
            pltpu.VMEM((3, grid_width, narrow), bf16),
            pltpu.SemaphoreType.DMA((count,)),
            pltpu.SemaphoreType.DMA((count,)),
            pltpu.SemaphoreType.DMA((5 + per * reduce_parts,)),
            pltpu.SemaphoreType.REGULAR((2,)),
        ],
        compiler_params=pltpu.CompilerParams(
            collective_id=0, has_side_effects=True, vmem_limit_bytes=VMEM_LIMIT
        ),
        cost_estimate=pl.CostEstimate(
            flops=flops, bytes_accessed=8 * channels * units, transcendentals=0
        ),
        name="block",
    )(
        activations,
        grad_branch,
        w_expand,
        reduce_source,
        kernel,
        bias,
        ln_gain.reshape(cols, 1, narrow),
        ln_bias.reshape(cols, 1, narrow),
        vectors,
        local_gain[None, :],
        layer_scale[None, :],
        b_reduce[None, :],
    )
    grad_mixed = grad_mixed.reshape(row_count, grid_width, narrow)
    top, bottom = halo(grad_mixed)
    grad_input = depthwise(grad_mixed, top, bottom, kernel, True, cotangent)
    return (block_out.reshape(row_count, grid_width, narrow), grad_input)


def solution(mesh):
    return jax.shard_map(
        body,
        mesh=mesh,
        in_specs=(
            P("row", None, "col"),
            P("row", None, "col"),
            P(None, None, "col"),
            P(),
            P(),
            P("row", "col"),
            P("col"),
            P("col", "row"),
            P("col"),
            P("col"),
        ),
        out_specs=(P("row", None, "col"), P("row", None, "col")),
        check_vma=False,
    )
```

```python
import functools

import jax
import jax.numpy as jnp
from jax import lax
from jax.experimental import pallas as pl
from jax.experimental.pallas import tpu as pltpu
from jax.sharding import PartitionSpec as P

H = 48
LANES = 128

epsilon = 1e-06
root_half = 0.7071067811865476
density_scale = 0.3989422804014327


def conv_kernel(flip, add, x_ref, top_ref, bottom_ref, k_ref, *rest):
    if add:
        add_ref, o_ref, field = rest
    else:
        o_ref, field = rest
    rows, width, lanes = x_ref.shape
    field[...] = jnp.zeros_like(field)
    field[0:3, 8 : 8 + width, :] = top_ref[...].astype(jnp.float32)
    field[3 : 3 + rows, 8 : 8 + width, :] = x_ref[...].astype(jnp.float32)
    field[3 + rows : 6 + rows, 8 : 8 + width, :] = bottom_ref[...].astype(jnp.float32)

    @pl.loop(0, rows)
    def _(r):
        total = jnp.zeros((width, lanes), jnp.float32)
        for a in range(7):
            for b in range(7):
                weight = k_ref[6 - a, 6 - b] if flip else k_ref[a, b]
                total += weight[None, :] * field[r + a, 5 + b : 5 + b + width, :]
        mixed = total.astype(jnp.bfloat16)
        if add:
            mixed = (add_ref[r].astype(jnp.float32) + mixed.astype(jnp.float32)).astype(
                jnp.bfloat16
            )
        o_ref[r] = mixed


def depthwise(field, top, bottom, kernel, flip, add=None):
    rows, width, channels = field.shape
    lanes = LANES if channels % LANES == 0 else channels
    block = lambda n: pl.BlockSpec((n, width, lanes), lambda i: (0, 0, i))
    operands = [field, top, bottom, kernel]
    specs = [block(rows), block(3), block(3), pl.BlockSpec((7, 7, lanes), lambda i: (0, 0, i))]
    if add is not None:
        operands.append(add)
        specs.append(block(rows))
    return pl.pallas_call(
        functools.partial(conv_kernel, flip, add is not None),
        out_shape=jax.ShapeDtypeStruct(field.shape, jnp.bfloat16),
        grid=(channels // lanes,),
        in_specs=specs,
        out_specs=block(rows),
        scratch_shapes=[pltpu.VMEM((rows + 6, width + 16, lanes), jnp.float32)],
        compiler_params=pltpu.CompilerParams(vmem_limit_bytes=32 * 2**20),
        cost_estimate=pl.CostEstimate(
            flops=98 * rows * width * channels,
            bytes_accessed=6 * rows * width * channels,
            transcendentals=0,
        ),
        name="depthwise_flipped" if flip else "depthwise",
    )(*operands)


def halo(field):
    rows = field.shape[0]
    per_image = H // rows
    count = lax.axis_size("row")
    down = [(i, i + 1) for i in range(count - 1) if (i + 1) % per_image]
    up = [(j, i) for i, j in down]
    return lax.ppermute(field[-3:], "row", down), lax.ppermute(field[:3], "row", up)


MESH = pl.DeviceIdType.MESH
VMEM_LIMIT = 127 * 2**19


def flip(index, bit):
    return index + bit - 2 * bit * ((index // bit) % 2)


def flip_all(index, mask):
    bit = 1
    while bit <= mask:
        if mask & bit:
            index = flip(index, bit)
        bit *= 2
    return index


def token_tile(tokens):
    for tile in (384, 192, 96, 48, 16):
        if tokens % tile == 0:
            return tile
    return tokens


def split_columns(narrow):
    if narrow % LANES:
        return [(0, narrow)]
    return [(start, LANES) for start in range(0, narrow, LANES)]


def block_kernel(
    rows,
    cols,
    act,
    grad,
    w_expand,
    w_reduce,
    taps,
    bias,
    gain,
    shift,
    vectors,
    local_gain,
    scale,
    b_reduce,
    out,
    grad_mixed,
    mixes,
    grads,
    stage,
    held,
    expand,
    reduce,
    hidden,
    slopes,
    preact,
    mixed,
    stats,
    units_in,
    sums,
    sums_in,
    top,
    bottom,
    send,
    recv,
    local,
    free,
):
    tokens, narrow = grad.shape
    width = top.shape[0] // 3
    row_count = tokens // width
    channels = narrow * cols
    depth, units = expand.shape[1:]
    per = depth // narrow
    sliced = narrow % LANES == 0
    tile = token_tile(tokens)
    tiles = tokens // tile
    small = min(tile, 192)
    per_image = H // row_count
    r, c = lax.axis_index("row"), lax.axis_index("col")
    parity = r % 2
    blocks = cols // 2
    bits = [1 << b for b in range(1, cols.bit_length() - 1)]
    steps = len(bits)
    second = bits[steps // 2 :] + bits[: steps // 2]
    f32, bf16 = jnp.float32, jnp.bfloat16
    dot = functools.partial(jnp.dot, preferred_element_type=f32)
    turned = lambda left, right: lax.dot_general(
        left, right, (((1,), (1,)), ((), ())), preferred_element_type=f32
    )
    row_of = lambda distance: (flip_all(r, distance), c)
    core = (r, flip(c, 1))
    partner = row_of(1)

    def step_column(index, half, s):
        e = (r + half) % 2
        return flip(index, bits[s]) * (1 - e) + flip(index, second[s]) * e

    def owner_of(half, j):
        index = c
        for s in range(steps):
            index = index + ((j // (1 << s)) % 2) * (step_column(index, half, s) - index)
        return index

    counter = [0]

    def new(count=1):
        counter[0] += count
        return counter[0] - count

    def remote(src, dst, sem, device):
        return pltpu.make_async_remote_copy(
            src_ref=src,
            dst_ref=dst,
            send_sem=send.at[sem],
            recv_sem=recv.at[sem],
            device_id=device,
            device_id_type=MESH,
        )

    barrier = pltpu.get_barrier_semaphore()
    others = [row_of(d) for d in range(1, rows)] + [(r, flip(c, bit)) for bit in [1] + bits]
    for device in others:
        pl.semaphore_signal(barrier, inc=1, device_id=device, device_id_type=MESH)
    pl.semaphore_wait(barrier, len(others))

    has_top, has_bottom = r % per_image != 0, (r + 1) % per_image != 0
    up_device = ((r + rows - 1) % rows, c)
    down_device = ((r + 1) % rows, c)
    down = remote(act.at[pl.ds(tokens - 3 * width, 3 * width)], top, new(), down_device)
    up = remote(act.at[pl.ds(0, 3 * width)], bottom, new(), up_device)
    if per_image > 1:
        pl.when(has_bottom)(down.start)
        pl.when(has_top)(up.start)

    def parts_of_expand(distance):
        half = (flip_all(r, distance) % 2) * units
        return w_expand.at[:, pl.ds(pl.multiple_of(half, units), units)]

    reduce_ranges = split_columns(narrow)

    def parts_of_reduce(distance, start, size):
        half = flip_all(r, distance) % 2
        pairs = []
        for i in range(per):
            if sliced:
                span = pl.ds(i * narrow + start, size)
                rows_of = pl.ds(pl.multiple_of(half * units, units), units)
                pairs.append((w_reduce.at[rows_of, span], reduce.at[r, :, span]))
            else:
                pairs.append((w_reduce.at[half, i], reduce.at[r * per + i]))
        return pairs

    def loads(pairs, base):
        copies = []
        for index, (src, dst) in enumerate(pairs):
            copies.append(pltpu.make_async_copy(src, dst, local.at[base + index]))
            copies[-1].start()
        return copies

    act_in = loads([(act, held)], 0)
    expand_own = loads([(parts_of_expand(0), expand.at[r])], 3)
    grad_own = loads([(grad, grads.at[0, c])], 4)

    expand_copies = [
        remote(parts_of_expand(d), expand.at[r], new(), row_of(d)) for d in range(rows - 1, 0, -1)
    ]

    sets = 2
    set_tokens = tokens // sets

    def gather(buffer, source):
        def there(half, j, q):
            span = pl.ds(q * set_tokens, set_tokens)
            order = (bits, second)[q]
            owner = c
            for s in range(steps):
                if (j >> s) & 1:
                    owner = flip(owner, order[s])
            target = buffer.at[half, owner, span]
            return (source.at[span] if half == 0 and j == 0 else target), target

        def step_copies(half, s, q):
            device = (r, flip(c, (bits, second)[q][s]))
            return [remote(*there(half, j, q), new(), device) for j in range(1 << s)]

        step_list = [
            [[step_copies(half, s, q) for q in range(sets)] for s in range(steps)]
            for half in (0, 1)
        ]
        across = []
        for q in range(sets):
            span = pl.ds(q * set_tokens, set_tokens)
            across.append(remote(source.at[span], buffer.at[1, c, span], new(), partner))
        core_list = [
            [[remote(*there(half, j, q), new(), core) for j in range(blocks)] for q in range(sets)]
            for half in (0, 1)
        ]
        return step_list, across, core_list

    grad_steps, grad_across, grad_core = gather(grads, grad)
    mix_steps, mix_across, mix_core = gather(mixes, mixed)

    def begin(copies):
        for copy in copies:
            copy.start()

    def arrive(copies):
        for copy in copies:
            copy.wait_recv()

    def leave(copies):
        for copy in copies:
            copy.wait_send()

    for q in range(sets):
        begin(grad_steps[0][0][q])
    begin(expand_copies[:1])
    reduce_own = loads(
        [pair for start, size in reduce_ranges for pair in parts_of_reduce(0, start, size)], 5
    )

    for copy in act_in:
        copy.wait()
    if per_image > 1:

        @pl.when(has_top)
        def _():
            down.wait_recv()

        @pl.when(has_bottom)
        def _():
            up.wait_recv()

    lanes = LANES if sliced else narrow
    pitch = preact.shape[1]

    def place(row, value):
        preact[row, 8 : 8 + width, 0:lanes] = value.astype(f32)

    for group in range(narrow // lanes):
        span = pl.ds(group * lanes, lanes)

        @pl.loop(0, row_count + 6)
        def _(i):
            preact[i, :, 0:lanes] = jnp.zeros((pitch, lanes), f32)

        @pl.loop(0, row_count)
        def _(i):
            place(i + 3, held[pl.ds(pl.multiple_of(i * width, 16), width), span])

        if per_image > 1:

            @pl.when(has_top)
            def _():
                for i in range(3):
                    place(i, top[i * width : (i + 1) * width, span])

            @pl.when(has_bottom)
            def _():
                for i in range(3):
                    place(i + row_count + 3, bottom[i * width : (i + 1) * width, span])

        @pl.loop(0, row_count)
        def _(i):
            total = jnp.zeros((width, lanes), f32)
            for a in range(7):
                for b in range(7):
                    total += (
                        taps[a, b, span][None, :]
                        * preact[i + a, 5 + b : 5 + b + width, 0:lanes]
                    )
            value = total.astype(bf16)
            mixed[pl.ds(pl.multiple_of(i * width, 16), width), span] = value

    begin(mix_across)
    for q in range(sets):
        begin(mix_steps[0][0][q])
    own_mixed = loads([(mixed, mixes.at[0, c])], 1)
    for q in range(sets):
        begin(mix_core[0][q][:1])
    for copy in own_mixed + grad_own:
        copy.wait()

    def advance(step_list, core_list, half, s):
        for q in range(sets):
            arrive(step_list[half][s][q])
            if s + 1 < steps:
                begin(step_list[half][s + 1][q])
            begin(core_list[half][q][1 << s : 2 << s])

    advance(mix_steps, mix_core, 0, 0)
    for q in range(sets):
        arrive(mix_across[q : q + 1])
        begin(mix_steps[1][0][q])
        begin(mix_core[1][q][:1])
    begin(expand_copies[1:-1])
    for s in range(1, steps):
        advance(mix_steps, mix_core, 0, s)
        advance(mix_steps, mix_core, 1, s - 1)
    advance(grad_steps, grad_core, 0, 0)
    begin(expand_copies[-1:])
    begin(grad_across)
    for q in range(sets):
        begin(grad_core[0][q][:1])
    advance(mix_steps, mix_core, 1, steps - 1)
    for q in range(sets):
        arrive(grad_across[q : q + 1])
        begin(grad_steps[1][0][q])
        begin(grad_core[1][q][:1])

    for copy in expand_own:
        copy.wait()
    arrive(expand_copies[:-1])
    for copy in reduce_own:
        copy.wait()
    reduce_copies = []
    for start, size in reduce_ranges:
        copies = []
        for d in range(rows - 1, 0, -1):
            copies += [
                remote(src, dst, new(), row_of(d)) for src, dst in parts_of_reduce(d, start, size)
            ]
        reduce_copies.append(copies)
    begin(reduce_copies[0])
    arrive(expand_copies[-1:])

    extra = jnp.zeros((vectors.shape[1], units), f32)
    for b in range(rows):
        extra += dot(vectors[b], expand[b])
    units_in[0:1, :] = extra[0:1] + extra[1:2] + extra[2:3]
    units_in[1:2, :] = bias[...] + (extra[3:4] + extra[4:5] + extra[5:6])

    def at(half, t, tile=tile):
        return pl.ds(pl.multiple_of(half * tokens + t * tile, 16), tile)

    def group_at(half, t, tile=tile):
        return pl.ds(half * (tokens // pitch) + t * (tile // pitch), tile // pitch)

    def expand_tokens(half):
        @pl.loop(0, tokens // small)
        def _(t):
            rows_at = pl.ds(pl.multiple_of(t * small, 16), small)
            total = jnp.zeros((small, 1), f32)
            square = jnp.zeros((small, 1), f32)
            for o in range(cols):
                value = mixes[half, o, rows_at, :].astype(f32)
                total += jnp.sum(value, 1, keepdims=True)
                square += jnp.sum(value * value, 1, keepdims=True)
            mean = total / channels
            inv = lax.rsqrt(square / channels - mean * mean + epsilon)
            if half == 0:
                stats[rows_at, 0:1] = mean
                stats[rows_at, 1:2] = inv
            value = jnp.zeros((small, units), f32) + bias[...]
            for b in range(rows):
                group = [b * per + i for i in range(per)]
                normed = [
                    (
                        (mixes[half, o, rows_at, :].astype(f32) - mean) * inv * gain[o] + shift[o]
                    ).astype(bf16)
                    for o in group
                ]
                if sliced:
                    value += dot(jnp.concatenate(normed, 1), expand[b])
                else:
                    for i in range(per):
                        value += dot(normed[i], expand[b, i * narrow : (i + 1) * narrow, :])
            cumulative = 0.5 * (1.0 + lax.erf(value * root_half))
            hidden[at(half, t, small), :] = (value * cumulative).astype(bf16)
            preact[group_at(half, t, small)] = value.reshape(-1, pitch, units)

    def arrive_core(core_list, half):
        for q in range(sets):
            arrive(core_list[half][q])

    arrive_core(mix_core, 0)
    expand_tokens(0)
    for s in range(1, steps):
        advance(grad_steps, grad_core, 0, s)
    advance(grad_steps, grad_core, 1, 0)
    arrive_core(mix_core, 1)
    expand_tokens(1)
    for s in range(1, steps):
        advance(grad_steps, grad_core, 1, s)

    nearby = [core, partner] + [(r, flip(c, bit)) for bit in bits]

    def release(index):
        for device in nearby:
            pl.semaphore_signal(free.at[index], inc=1, device_id=device, device_id_type=MESH)

    def leave_gather(step_list, across, core_list):
        leave(across)
        for half in (0, 1):
            for q in range(sets):
                leave(core_list[half][q])
                for s in range(steps):
                    leave(step_list[half][s][q])

    leave_gather(mix_steps, mix_across, mix_core)
    release(0)

    def sum_part(buffer, part, columns, tile_range, emit, stage=stage):
        base = new(4 * blocks - 1)
        start, size = columns[:2]
        span = pl.ds(start, size)
        stage_span = pl.ds(columns[-1] if len(columns) > 2 else start, size)
        first_tile, tile_count = tile_range
        here = pl.ds(first_tile * tile, tile_count * tile)

        def core_copy(half, j, slot):
            return remote(
                stage.at[slot, here, stage_span],
                buffer.at[half, j, here, span],
                base + half * blocks + j,
                core,
            )

        def step_copy(half, s, i):
            return remote(
                stage.at[2 * ((1 << s) - 1) + 2 * i + half, here, stage_span],
                buffer.at[half, blocks + (1 << s) - 1 + i, here, span],
                base + 2 * blocks + 2 * ((1 << s) - 1) + 2 * i + half,
                (r, step_column(c, half, s)),
            )

        pair_copy = remote(
            stage.at[2 * (blocks - 1), here, stage_span],
            buffer.at[0, cols - 1, here, span],
            base + 4 * blocks - 2,
            partner,
        )

        def total(half, t, owner, j, later):
            rows_at = pl.ds(pl.multiple_of(t * tile, 16), tile)
            value = part(half, t, owner, start, size)
            value += buffer[half, j, rows_at, span].astype(f32)
            for s in later:
                value += buffer[half, blocks + (1 << s) - 1 + j, rows_at, span].astype(f32)
            return value

        def over_tiles(slot, value_of):
            @pl.loop(first_tile, first_tile + tile_count)
            def _(t):
                rows_at = pl.ds(pl.multiple_of(t * tile, 16), tile)
                stage[slot, rows_at, stage_span] = value_of(t).astype(bf16)

        def first():
            @pl.loop(0, 2 * blocks)
            def _(i):
                half, j = i % 2, blocks - 1 - i // 2
                owner = flip(owner_of(half, j), 1)
                over_tiles(i, lambda t: part(half, t, owner, start, size))
                core_copy(half, j, i).start()

        def clear():
            @pl.loop(0, 2 * blocks)
            def _(i):
                core_copy(i % 2, blocks - 1 - i // 2, i).wait_send()

        def step(s):
            @pl.loop(0, 2 << s)
            def _(n):
                half, i = n % 2, n // 2
                j = i + (1 << s)
                core_copy(half, j, 0).wait_recv()
                for later in range(s + 1, steps):
                    step_copy(half, later, j).wait_recv()
                owner = owner_of(half, j)
                over_tiles(
                    2 * ((1 << s) - 1) + n,
                    lambda t: total(half, t, owner, j, range(s + 1, steps)),
                )
                step_copy(half, s, i).start()

        def across():
            core_copy(1, 0, 0).wait_recv()
            for s in range(steps):
                step_copy(1, s, 0).wait_recv()
            over_tiles(2 * (blocks - 1), lambda t: total(1, t, c, 0, range(steps)))
            pair_copy.start()

        def last():
            core_copy(0, 0, 0).wait_recv()
            for s in range(steps):
                step_copy(0, s, 0).wait_recv()
            pair_copy.wait_recv()

            @pl.loop(first_tile, first_tile + tile_count)
            def _(t):
                rows_at = pl.ds(pl.multiple_of(t * tile, 16), tile)
                value = total(0, t, c, 0, range(steps))
                value += buffer[0, cols - 1, rows_at, span].astype(f32)
                emit(t, rows_at, span, start, size, value)

        def finish():
            for s in range(steps):

                @pl.loop(0, 2 << s)
                def _(n):
                    step_copy(n % 2, s, n // 2).wait_send()

            pair_copy.wait_send()

        def step_cleared(s):
            if s == steps - 1:
                clear()
            step(s)

        turns = [functools.partial(step_cleared, s) for s in range(steps - 1, -1, -1)]
        return [first] + turns + [across, last, finish]

    def branch_part(half, t, owner, start, size):
        if sliced:
            at_lane = pl.multiple_of((owner % per) * narrow + start, LANES)
            weights = reduce[owner // per, :, pl.ds(at_lane, size)]
        else:
            weights = reduce[owner]
        return dot(hidden[at(half, t), :], weights)

    def grad_part(half, t, owner, start, size):
        at_row = pl.multiple_of((owner % per) * narrow + start, 16)
        return turned(slopes[at(half, t), :], expand[owner // per, pl.ds(at_row, size), :])

    def emit_branch(t, rows_at, span, start, size, value):
        lane = slice(start, start + size)
        value = scale[:, lane] * (value + b_reduce[:, lane])
        held[rows_at, span] = (held[rows_at, span].astype(f32) + value).astype(bf16)

    def emit_grad(t, rows_at, span, start, size, value):
        lane = slice(start, start + size)
        mean, inv = stats[rows_at, 0:1], stats[rows_at, 1:2]
        both = jnp.transpose(sums[0, t])
        normal = (mixed[rows_at, span].astype(f32) - mean) * inv
        value = value * local_gain[:, lane]
        value = inv * (value - both[:, 0:1] / channels - normal * both[:, 1:2] / channels)
        mixed[rows_at, span] = value.astype(bf16)

    def grad_tokens(t):
        @pl.loop(0, 2)
        def _(half):
            rows_at = pl.ds(pl.multiple_of(t * tile, 16), tile)
            value = jnp.zeros((tile, units), f32)
            for b in range(rows):
                group = [grads[half, b * per + i, rows_at, :] for i in range(per)]
                if sliced:
                    value += turned(jnp.concatenate(group, 1), reduce[b])
                else:
                    for i in range(per):
                        value += turned(group[i], reduce[b * per + i])
            a = preact[group_at(half, t)].reshape(tile, units)
            cumulative = 0.5 * (1.0 + lax.erf(a * root_half))
            slope = cumulative + a * jnp.exp(-0.5 * a * a) * density_scale
            rounded = (value * slope).astype(bf16)
            slopes[at(half, t), :] = rounded
            rounded = rounded.astype(f32)
            total = jnp.sum(rounded * units_in[0:1, :], 1, keepdims=True)
            cross = jnp.sum(rounded * (a - units_in[1:2, :]), 1, keepdims=True)
            lane = lax.broadcasted_iota(jnp.int32, (tile, LANES), 1)
            both = jnp.where(lane == 0, total, jnp.where(lane == 1, cross, 0.0))
            sums[half, t] = jnp.transpose(both)[0:8]

    pl.semaphore_wait(free.at[0], len(nearby))
    branch_units = []
    for index, (start, size) in enumerate(reduce_ranges):
        columns, where = (start, size), stage
        if index == len(reduce_ranges) - 1 and index >= 2:
            columns, where = (start, size, reduce_ranges[0][0]), mixes.at[0]
        branch_units.append(
            sum_part(mixes, branch_part, columns, (0, tiles), emit_branch, where)
        )
    first_index, turn, across_index, last_index = 0, 1, 1 + steps, 2 + steps
    spare = len(branch_units) >= 3
    arrive(reduce_copies[0])
    begin([copy for copies in reduce_copies[1:2] for copy in copies])
    for index, unit in enumerate(branch_units):
        if index:
            arrive(reduce_copies[index])
            begin([copy for copies in reduce_copies[index + 1 : index + 2] for copy in copies])
            before = branch_units[index - 1]
            for s in range(1, steps):
                before[turn + s]()
            if spare and index == len(branch_units) - 1:
                for done in branch_units[: index - 1]:
                    done[last_index]()
        unit[first_index]()
        if index:
            before[across_index]()
        unit[turn]()

    arrive_core(grad_core, 0)
    arrive_core(grad_core, 1)
    leave_gather(grad_steps, grad_across, grad_core)
    latest = branch_units[-1]
    for unit in branch_units[:-1]:
        unit[-1]()

    def finish_latest():
        for s in range(1, steps):
            latest[turn + s]()

    sum_devices = [partner] + [(r, flip(c, bit)) for bit in [1] + bits]
    sum_copies = [
        remote(sums.at[1 if n == 0 else 0], sums_in.at[n], new(), device)
        for n, device in enumerate(sum_devices)
    ]

    def sum_step(n):
        if 0 < n <= len(sum_copies):
            sum_copies[n - 1].wait()
            sums[0] = sums[0] + sums_in[n - 1]
        if n < len(sum_copies):
            sum_copies[n].start()

    grad_units = [sum_part(grads, grad_part, (0, narrow), (t, 1), emit_grad) for t in range(tiles)]

    if not spare:
        finish_latest()
        latest[across_index]()
        latest[-1]()
    for t, unit in enumerate(grad_units):
        grad_tokens(t)
        release(1 + t)
        if t == tiles - 1:
            sum_step(0)
        if t:
            grad_units[t - 1][turn]()
        pl.semaphore_wait(free.at[1 + t], len(nearby))
        unit[first_index]()
        if spare and t == 0:
            finish_latest()
        if spare and t == min(1, tiles - 1):
            latest[across_index]()
    grad_units[-1][turn]()
    sum_index = 1
    for t, unit in enumerate(grad_units):
        for s in range(1, steps):
            unit[turn + s]()
        if t:
            grad_units[t - 1][across_index]()
        sum_step(sum_index)
        sum_index += 1
    grad_units[-1][across_index]()
    while sum_index <= len(sum_copies):
        sum_step(sum_index)
        sum_index += 1
    for unit in branch_units[-2:] if spare else branch_units:
        unit[last_index]()
    out_copy = pltpu.make_async_copy(held, out, local.at[0])
    out_copy.start()
    for unit in grad_units:
        unit[last_index]()
    grad_copy = pltpu.make_async_copy(mixed, grad_mixed, local.at[1])
    grad_copy.start()
    if spare:
        latest[-1]()
    for unit in grad_units:
        unit[-1]()
    out_copy.wait()
    grad_copy.wait()

    leave(expand_copies)
    for copies in reduce_copies:
        leave(copies)
    if per_image > 1:
        pl.when(has_bottom)(down.wait_send)
        pl.when(has_top)(up.wait_send)


def semaphores_needed(rows, cols, per, reduce_parts, grad_parts):
    blocks, steps = cols // 2, cols.bit_length() - 2
    gathers = 4 * (2 * (blocks - 1) + 1 + 2 * blocks)
    weights = (rows - 1) * (1 + per * reduce_parts)
    return 2 + weights + gathers + (reduce_parts + grad_parts) * (4 * blocks - 1) + steps + 2


def body(
    activations,
    cotangent,
    kernel,
    ln_gain,
    ln_bias,
    w_expand,
    b_expand,
    w_reduce,
    b_reduce,
    layer_scale,
):
    row_count, grid_width, narrow = activations.shape
    rows, cols = lax.axis_size("row"), lax.axis_size("col")
    me_row, me_col = lax.axis_index("row"), lax.axis_index("col")
    channels = narrow * cols
    depth = channels // rows
    per = depth // narrow
    tokens = row_count * grid_width
    units = w_expand.shape[1] // 2
    sliced = narrow % LANES == 0
    tile = token_tile(tokens)
    f32, bf16 = jnp.float32, jnp.bfloat16

    cot_f = cotangent.astype(f32)
    grad_branch = (layer_scale * cot_f).reshape(tokens, narrow).astype(bf16)
    bias = lax.dynamic_slice_in_dim(b_expand, (me_row % 2) * units, units)[None, :]
    exact = []
    for vector in (ln_gain, ln_bias):
        for _ in range(3):
            piece = lax.reduce_precision(vector, 8, 7)
            exact.append(piece.astype(bf16))
            vector = vector - piece
    exact += [jnp.zeros_like(exact[0])] * (16 - len(exact))
    vectors = jnp.stack(exact).reshape(16, rows, depth).transpose(1, 0, 2)
    if sliced:
        reduce_source = w_reduce
        reduce_shape = (rows, units, depth)
    else:
        reduce_source = w_reduce.reshape(2, units, per, narrow).transpose(0, 2, 1, 3)
        reduce_shape = (cols, units, narrow)
    local_gain = lax.dynamic_slice_in_dim(ln_gain, me_col * narrow, narrow)
    reduce_parts = len(split_columns(narrow))
    count = semaphores_needed(rows, cols, per, reduce_parts, tokens // tile)
    steps = cols.bit_length() - 2

    anywhere = pl.BlockSpec(memory_space=pl.ANY)
    inside = pl.BlockSpec(memory_space=pltpu.VMEM)
    flops = 8 * 2 * tokens * channels * units
    block_out, grad_mixed = pl.pallas_call(
        functools.partial(block_kernel, rows, cols),
        out_shape=[jax.ShapeDtypeStruct((tokens, narrow), bf16)] * 2,
        in_specs=[anywhere] * 4 + [inside] * 8,
        out_specs=[anywhere] * 2,
        scratch_shapes=[
            pltpu.VMEM((2, cols, tokens, narrow), bf16),
            pltpu.VMEM((2, cols, tokens, narrow), bf16),
            pltpu.VMEM((cols, tokens, narrow), bf16),
            pltpu.VMEM((tokens, narrow), bf16),
            pltpu.VMEM((rows, depth, units), bf16),
            pltpu.VMEM(reduce_shape, bf16),
            pltpu.VMEM((2 * tokens, units), bf16),
            pltpu.VMEM((2 * tokens, units), bf16),
            pltpu.VMEM((2 * tokens // (grid_width + 16), grid_width + 16, units), f32),
            pltpu.VMEM((tokens, narrow), bf16),
            pltpu.VMEM((tokens, 2), f32),
            pltpu.VMEM((2, units), f32),
            pltpu.VMEM((2, tokens // tile, 8, tile), f32),
            pltpu.VMEM((steps + 2, tokens // tile, 8, tile), f32),
            pltpu.VMEM((3 * grid_width, narrow), bf16),
            pltpu.VMEM((3 * grid_width, narrow), bf16),
            pltpu.SemaphoreType.DMA((count,)),
            pltpu.SemaphoreType.DMA((count,)),
            pltpu.SemaphoreType.DMA((5 + per * reduce_parts,)),
            pltpu.SemaphoreType.REGULAR((1 + tokens // tile,)),
        ],
        compiler_params=pltpu.CompilerParams(
            collective_id=0, has_side_effects=True, vmem_limit_bytes=VMEM_LIMIT
        ),
        cost_estimate=pl.CostEstimate(
            flops=flops, bytes_accessed=8 * channels * units, transcendentals=0
        ),
        name="block",
    )(
        activations.reshape(tokens, narrow),
        grad_branch,
        w_expand,
        reduce_source,
        kernel,
        bias,
        ln_gain.reshape(cols, 1, narrow),
        ln_bias.reshape(cols, 1, narrow),
        vectors,
        local_gain[None, :],
        layer_scale[None, :],
        b_reduce[None, :],
    )
    grad_mixed = grad_mixed.reshape(row_count, grid_width, narrow)
    top, bottom = halo(grad_mixed)
    grad_input = depthwise(grad_mixed, top, bottom, kernel, True, cotangent)
    return (block_out.reshape(row_count, grid_width, narrow), grad_input)


def solution(mesh):
    return jax.shard_map(
        body,
        mesh=mesh,
        in_specs=(
            P("row", None, "col"),
            P("row", None, "col"),
            P(None, None, "col"),
            P(),
            P(),
            P("row", "col"),
            P("col"),
            P("col", "row"),
            P("col"),
            P("col"),
        ),
        out_specs=(P("row", None, "col"), P("row", None, "col")),
        check_vma=False,
    )
```

```python
import functools

import jax
import jax.numpy as jnp
from jax import lax
from jax.experimental import pallas as pl
from jax.experimental.pallas import tpu as pltpu
from jax.sharding import PartitionSpec as P

H = 48
LANES = 128

epsilon = 1e-06
root_half = 0.7071067811865476
density_scale = 0.3989422804014327


def conv_kernel(flip, add, x_ref, top_ref, bottom_ref, k_ref, *rest):
    if add:
        add_ref, o_ref, field = rest
    else:
        o_ref, field = rest
    rows, width, lanes = x_ref.shape
    field[...] = jnp.zeros_like(field)
    field[0:3, 8 : 8 + width, :] = top_ref[...].astype(jnp.float32)
    field[3 : 3 + rows, 8 : 8 + width, :] = x_ref[...].astype(jnp.float32)
    field[3 + rows : 6 + rows, 8 : 8 + width, :] = bottom_ref[...].astype(jnp.float32)

    @pl.loop(0, rows)
    def _(r):
        total = jnp.zeros((width, lanes), jnp.float32)
        for a in range(7):
            for b in range(7):
                weight = k_ref[6 - a, 6 - b] if flip else k_ref[a, b]
                total += weight[None, :] * field[r + a, 5 + b : 5 + b + width, :]
        mixed = total.astype(jnp.bfloat16)
        if add:
            mixed = (add_ref[r].astype(jnp.float32) + mixed.astype(jnp.float32)).astype(
                jnp.bfloat16
            )
        o_ref[r] = mixed


def depthwise(field, top, bottom, kernel, flip, add=None):
    rows, width, channels = field.shape
    lanes = LANES if channels % LANES == 0 else channels
    block = lambda n: pl.BlockSpec((n, width, lanes), lambda i: (0, 0, i))
    operands = [field, top, bottom, kernel]
    specs = [block(rows), block(3), block(3), pl.BlockSpec((7, 7, lanes), lambda i: (0, 0, i))]
    if add is not None:
        operands.append(add)
        specs.append(block(rows))
    return pl.pallas_call(
        functools.partial(conv_kernel, flip, add is not None),
        out_shape=jax.ShapeDtypeStruct(field.shape, jnp.bfloat16),
        grid=(channels // lanes,),
        in_specs=specs,
        out_specs=block(rows),
        scratch_shapes=[pltpu.VMEM((rows + 6, width + 16, lanes), jnp.float32)],
        compiler_params=pltpu.CompilerParams(vmem_limit_bytes=32 * 2**20),
        cost_estimate=pl.CostEstimate(
            flops=98 * rows * width * channels,
            bytes_accessed=6 * rows * width * channels,
            transcendentals=0,
        ),
        name="depthwise_flipped" if flip else "depthwise",
    )(*operands)


def halo(field):
    rows = field.shape[0]
    per_image = H // rows
    count = lax.axis_size("row")
    down = [(i, i + 1) for i in range(count - 1) if (i + 1) % per_image]
    up = [(j, i) for i, j in down]
    return lax.ppermute(field[-3:], "row", down), lax.ppermute(field[:3], "row", up)


MESH = pl.DeviceIdType.MESH
VMEM_LIMIT = 127 * 2**19


def flip(index, bit):
    return index + bit - 2 * bit * ((index // bit) % 2)


def flip_all(index, mask):
    bit = 1
    while bit <= mask:
        if mask & bit:
            index = flip(index, bit)
        bit *= 2
    return index


def token_tile(tokens):
    for tile in (384, 192, 96, 48, 16):
        if tokens % tile == 0:
            return tile
    return tokens


def split_columns(narrow):
    if narrow % LANES:
        return [(0, narrow)]
    return [(start, LANES) for start in range(0, narrow, LANES)]


def block_kernel(
    rows,
    cols,
    act,
    grad,
    w_expand,
    w_reduce,
    taps,
    bias,
    gain,
    shift,
    local_gain,
    scale,
    b_reduce,
    out,
    grad_mixed,
    mixes,
    grads,
    stage,
    held,
    expand,
    reduce,
    hidden,
    slopes,
    preact,
    mixed,
    stats,
    units_in,
    sums,
    sums_in,
    top,
    bottom,
    send,
    recv,
    local,
    free,
):
    tokens, narrow = grad.shape
    width = top.shape[0] // 3
    row_count = tokens // width
    channels = narrow * cols
    depth, units = expand.shape[1:]
    per = depth // narrow
    sliced = narrow % LANES == 0
    tile = token_tile(tokens)
    tiles = tokens // tile
    small = min(tile, 192)
    per_image = H // row_count
    r, c = lax.axis_index("row"), lax.axis_index("col")
    parity = r % 2
    blocks = cols // 2
    bits = [1 << b for b in range(1, cols.bit_length() - 1)]
    steps = len(bits)
    second = bits[steps // 2 :] + bits[: steps // 2]
    f32, bf16 = jnp.float32, jnp.bfloat16
    dot = functools.partial(jnp.dot, preferred_element_type=f32)
    turned = lambda left, right: lax.dot_general(
        left, right, (((1,), (1,)), ((), ())), preferred_element_type=f32
    )
    row_of = lambda distance: (flip_all(r, distance), c)
    core = (r, flip(c, 1))
    partner = row_of(1)

    def step_column(index, half, s):
        e = (r + half) % 2
        return flip(index, bits[s]) * (1 - e) + flip(index, second[s]) * e

    def owner_of(half, j):
        index = c
        for s in range(steps):
            index = index + ((j // (1 << s)) % 2) * (step_column(index, half, s) - index)
        return index

    counter = [0]

    def new(count=1):
        counter[0] += count
        return counter[0] - count

    def remote(src, dst, sem, device):
        return pltpu.make_async_remote_copy(
            src_ref=src,
            dst_ref=dst,
            send_sem=send.at[sem],
            recv_sem=recv.at[sem],
            device_id=device,
            device_id_type=MESH,
        )

    barrier = pltpu.get_barrier_semaphore()
    others = [row_of(d) for d in range(1, rows)] + [(r, flip(c, bit)) for bit in [1] + bits]
    for device in others:
        pl.semaphore_signal(barrier, inc=1, device_id=device, device_id_type=MESH)
    pl.semaphore_wait(barrier, len(others))

    has_top, has_bottom = r % per_image != 0, (r + 1) % per_image != 0
    up_device = ((r + rows - 1) % rows, c)
    down_device = ((r + 1) % rows, c)
    down = remote(act.at[pl.ds(tokens - 3 * width, 3 * width)], top, new(), down_device)
    up = remote(act.at[pl.ds(0, 3 * width)], bottom, new(), up_device)
    if per_image > 1:
        pl.when(has_bottom)(down.start)
        pl.when(has_top)(up.start)

    def parts_of_expand(distance):
        half = (flip_all(r, distance) % 2) * units
        return w_expand.at[:, pl.ds(pl.multiple_of(half, units), units)]

    reduce_ranges = split_columns(narrow)

    def parts_of_reduce(distance, start, size):
        half = flip_all(r, distance) % 2
        pairs = []
        for i in range(per):
            if sliced:
                span = pl.ds(i * narrow + start, size)
                rows_of = pl.ds(pl.multiple_of(half * units, units), units)
                pairs.append((w_reduce.at[rows_of, span], reduce.at[r, :, span]))
            else:
                pairs.append((w_reduce.at[half, i], reduce.at[r * per + i]))
        return pairs

    def loads(pairs, base):
        copies = []
        for index, (src, dst) in enumerate(pairs):
            copies.append(pltpu.make_async_copy(src, dst, local.at[base + index]))
            copies[-1].start()
        return copies

    act_in = loads([(act, held)], 0)
    expand_own = loads([(parts_of_expand(0), expand.at[r])], 3)
    grad_own = loads([(grad, grads.at[0, c])], 4)

    expand_copies = [
        remote(parts_of_expand(d), expand.at[r], new(), row_of(d)) for d in range(rows - 1, 0, -1)
    ]

    sets = 2
    set_tokens = tokens // sets

    def gather(buffer, source):
        def there(half, j, q):
            span = pl.ds(q * set_tokens, set_tokens)
            order = (bits, second)[q]
            owner = c
            for s in range(steps):
                if (j >> s) & 1:
                    owner = flip(owner, order[s])
            target = buffer.at[half, owner, span]
            return (source.at[span] if half == 0 and j == 0 else target), target

        def step_copies(half, s, q):
            device = (r, flip(c, (bits, second)[q][s]))
            return [remote(*there(half, j, q), new(), device) for j in range(1 << s)]

        step_list = [
            [[step_copies(half, s, q) for q in range(sets)] for s in range(steps)]
            for half in (0, 1)
        ]
        across = []
        for q in range(sets):
            span = pl.ds(q * set_tokens, set_tokens)
            across.append(remote(source.at[span], buffer.at[1, c, span], new(), partner))
        core_list = [
            [[remote(*there(half, j, q), new(), core) for j in range(blocks)] for q in range(sets)]
            for half in (0, 1)
        ]
        return step_list, across, core_list

    grad_steps, grad_across, grad_core = gather(grads, grad)
    mix_steps, mix_across, mix_core = gather(mixes, mixed)

    reduce_copies = []
    for start, size in reduce_ranges:
        copies = []
        for d in range(rows - 1, 0, -1):
            copies += [
                remote(src, dst, new(), row_of(d)) for src, dst in parts_of_reduce(d, start, size)
            ]
        reduce_copies.append(copies)

    def begin(copies):
        for copy in copies:
            copy.start()

    def arrive(copies):
        for copy in copies:
            copy.wait_recv()

    def leave(copies):
        for copy in copies:
            copy.wait_send()

    for q in range(sets):
        begin(grad_steps[0][0][q])
    begin(expand_copies[:1])
    reduce_own = loads(
        [pair for start, size in reduce_ranges for pair in parts_of_reduce(0, start, size)], 5
    )

    for copy in act_in:
        copy.wait()
    if per_image > 1:

        @pl.when(has_top)
        def _():
            down.wait_recv()

        @pl.when(has_bottom)
        def _():
            up.wait_recv()

    lanes = LANES if sliced else narrow
    pitch = preact.shape[1]

    def place(row, value):
        preact[row, 8 : 8 + width, 0:lanes] = value.astype(f32)

    for group in range(narrow // lanes):
        span = pl.ds(group * lanes, lanes)

        @pl.loop(0, row_count + 6)
        def _(i):
            preact[i, :, 0:lanes] = jnp.zeros((pitch, lanes), f32)

        @pl.loop(0, row_count)
        def _(i):
            place(i + 3, held[pl.ds(pl.multiple_of(i * width, 16), width), span])

        if per_image > 1:

            @pl.when(has_top)
            def _():
                for i in range(3):
                    place(i, top[i * width : (i + 1) * width, span])

            @pl.when(has_bottom)
            def _():
                for i in range(3):
                    place(i + row_count + 3, bottom[i * width : (i + 1) * width, span])

        @pl.loop(0, row_count)
        def _(i):
            total = jnp.zeros((width, lanes), f32)
            for a in range(7):
                for b in range(7):
                    total += (
                        taps[a, b, span][None, :]
                        * preact[i + a, 5 + b : 5 + b + width, 0:lanes]
                    )
            value = total.astype(bf16)
            mixed[pl.ds(pl.multiple_of(i * width, 16), width), span] = value

    begin(mix_across)
    for q in range(sets):
        begin(mix_steps[0][0][q])
    own_mixed = loads([(mixed, mixes.at[0, c])], 1)
    for q in range(sets):
        begin(mix_core[0][q][:1])
    for copy in own_mixed + grad_own:
        copy.wait()

    def advance(step_list, core_list, half, s):
        for q in range(sets):
            arrive(step_list[half][s][q])
            if s + 1 < steps:
                begin(step_list[half][s + 1][q])
            begin(core_list[half][q][1 << s : 2 << s])

    advance(mix_steps, mix_core, 0, 0)
    for q in range(sets):
        arrive(mix_across[q : q + 1])
        begin(mix_steps[1][0][q])
        begin(mix_core[1][q][:1])
        if q == 0:
            begin(expand_copies[1:-1])
    begin(grad_across)
    begin(expand_copies[-1:])
    for s in range(1, steps):
        advance(mix_steps, mix_core, 0, s)
        advance(mix_steps, mix_core, 1, s - 1)
    advance(mix_steps, mix_core, 1, steps - 1)
    advance(grad_steps, grad_core, 0, 0)
    for q in range(sets):
        begin(grad_core[0][q][:1])
    for q in range(sets):
        arrive(grad_across[q : q + 1])
        begin(grad_steps[1][0][q])
        begin(grad_core[1][q][:1])
    for copy in reduce_own + expand_own:
        copy.wait()
    begin(reduce_copies[0])
    arrive(expand_copies)

    extra = jnp.zeros((16, units), f32)
    for o in range(cols):
        exact = []
        for vector in (gain[o], shift[o]):
            for _ in range(3):
                piece = vector.astype(bf16).astype(f32)
                exact.append(piece)
                vector = vector - piece
        exact.append(jnp.zeros((16 - len(exact), narrow), f32))
        exact = jnp.concatenate(exact, 0).astype(bf16)
        lane = (o % per) * narrow
        extra += dot(exact, expand[o // per, lane : lane + narrow, :])
    units_in[0:1, :] = extra[0:1] + extra[1:2] + extra[2:3]
    units_in[1:2, :] = bias[...] + (extra[3:4] + extra[4:5] + extra[5:6])

    def at(half, t, tile=tile):
        return pl.ds(pl.multiple_of(half * tokens + t * tile, 16), tile)

    def group_at(half, t, tile=tile):
        return pl.ds(half * (tokens // pitch) + t * (tile // pitch), tile // pitch)

    def expand_tokens(half):
        @pl.loop(0, tokens // small)
        def _(t):
            rows_at = pl.ds(pl.multiple_of(t * small, 16), small)
            total = jnp.zeros((small, 1), f32)
            square = jnp.zeros((small, 1), f32)
            for o in range(cols):
                value = mixes[half, o, rows_at, :].astype(f32)
                total += jnp.sum(value, 1, keepdims=True)
                square += jnp.sum(value * value, 1, keepdims=True)
            mean = total / channels
            inv = lax.rsqrt(square / channels - mean * mean + epsilon)
            if half == 0:
                stats[rows_at, 0:1] = mean
                stats[rows_at, 1:2] = inv
            value = jnp.zeros((small, units), f32) + bias[...]
            for b in range(rows):
                group = [b * per + i for i in range(per)]
                normed = [
                    (
                        (mixes[half, o, rows_at, :].astype(f32) - mean) * inv * gain[o] + shift[o]
                    ).astype(bf16)
                    for o in group
                ]
                if sliced:
                    value += dot(jnp.concatenate(normed, 1), expand[b])
                else:
                    for i in range(per):
                        value += dot(normed[i], expand[b, i * narrow : (i + 1) * narrow, :])
            cumulative = 0.5 * (1.0 + lax.erf(value * root_half))
            hidden[at(half, t, small), :] = (value * cumulative).astype(bf16)
            preact[group_at(half, t, small)] = value.reshape(-1, pitch, units)

    def arrive_core(core_list, half):
        for q in range(sets):
            arrive(core_list[half][q])

    arrive_core(mix_core, 0)
    expand_tokens(0)
    for copies in reduce_copies[1:2]:
        begin(copies)
    for s in range(1, steps):
        advance(grad_steps, grad_core, 0, s)
    advance(grad_steps, grad_core, 1, 0)
    arrive_core(mix_core, 1)
    expand_tokens(1)
    for copies in reduce_copies[2:]:
        begin(copies)
    for s in range(1, steps):
        advance(grad_steps, grad_core, 1, s)

    nearby = [core, partner] + [(r, flip(c, bit)) for bit in bits]

    def release(index):
        for device in nearby:
            pl.semaphore_signal(free.at[index], inc=1, device_id=device, device_id_type=MESH)

    def leave_gather(step_list, across, core_list):
        leave(across)
        for half in (0, 1):
            for q in range(sets):
                leave(core_list[half][q])
                for s in range(steps):
                    leave(step_list[half][s][q])

    leave_gather(mix_steps, mix_across, mix_core)
    release(0)

    def sum_part(buffer, part, columns, tile_range, emit, stage=stage):
        base = new(4 * blocks - 1)
        start, size = columns[:2]
        span = pl.ds(start, size)
        stage_span = pl.ds(columns[-1] if len(columns) > 2 else start, size)
        first_tile, tile_count = tile_range
        here = pl.ds(first_tile * tile, tile_count * tile)

        def core_copy(half, j, slot):
            return remote(
                stage.at[slot, here, stage_span],
                buffer.at[half, j, here, span],
                base + half * blocks + j,
                core,
            )

        def step_copy(half, s, i):
            return remote(
                stage.at[2 * ((1 << s) - 1) + 2 * i + half, here, stage_span],
                buffer.at[half, blocks + (1 << s) - 1 + i, here, span],
                base + 2 * blocks + 2 * ((1 << s) - 1) + 2 * i + half,
                (r, step_column(c, half, s)),
            )

        pair_copy = remote(
            stage.at[2 * (blocks - 1), here, stage_span],
            buffer.at[0, cols - 1, here, span],
            base + 4 * blocks - 2,
            partner,
        )

        def total(half, t, owner, j, later):
            rows_at = pl.ds(pl.multiple_of(t * tile, 16), tile)
            value = part(half, t, owner, start, size)
            value += buffer[half, j, rows_at, span].astype(f32)
            for s in later:
                value += buffer[half, blocks + (1 << s) - 1 + j, rows_at, span].astype(f32)
            return value

        def over_tiles(slot, value_of):
            @pl.loop(first_tile, first_tile + tile_count)
            def _(t):
                rows_at = pl.ds(pl.multiple_of(t * tile, 16), tile)
                stage[slot, rows_at, stage_span] = value_of(t).astype(bf16)

        def first():
            @pl.loop(0, 2 * blocks)
            def _(i):
                half, j = i % 2, blocks - 1 - i // 2
                owner = flip(owner_of(half, j), 1)
                over_tiles(i, lambda t: part(half, t, owner, start, size))
                core_copy(half, j, i).start()

        def clear():
            @pl.loop(0, 2 * blocks)
            def _(i):
                core_copy(i % 2, blocks - 1 - i // 2, i).wait_send()

        def step(s):
            @pl.loop(0, 2 << s)
            def _(n):
                half, i = n % 2, n // 2
                j = i + (1 << s)
                core_copy(half, j, 0).wait_recv()
                for later in range(s + 1, steps):
                    step_copy(half, later, j).wait_recv()
                owner = owner_of(half, j)
                over_tiles(
                    2 * ((1 << s) - 1) + n,
                    lambda t: total(half, t, owner, j, range(s + 1, steps)),
                )
                step_copy(half, s, i).start()

        def across():
            core_copy(1, 0, 0).wait_recv()
            for s in range(steps):
                step_copy(1, s, 0).wait_recv()
            over_tiles(2 * (blocks - 1), lambda t: total(1, t, c, 0, range(steps)))
            pair_copy.start()

        def last():
            core_copy(0, 0, 0).wait_recv()
            for s in range(steps):
                step_copy(0, s, 0).wait_recv()
            pair_copy.wait_recv()

            @pl.loop(first_tile, first_tile + tile_count)
            def _(t):
                rows_at = pl.ds(pl.multiple_of(t * tile, 16), tile)
                value = total(0, t, c, 0, range(steps))
                value += buffer[0, cols - 1, rows_at, span].astype(f32)
                emit(t, rows_at, span, start, size, value)

        def finish():
            for s in range(steps):

                @pl.loop(0, 2 << s)
                def _(n):
                    step_copy(n % 2, s, n // 2).wait_send()

            pair_copy.wait_send()

        def step_cleared(s):
            if s == steps - 1:
                clear()
            step(s)

        turns = [functools.partial(step_cleared, s) for s in range(steps - 1, -1, -1)]
        return [first] + turns + [across, last, finish]

    def branch_part(half, t, owner, start, size):
        if sliced:
            at_lane = pl.multiple_of((owner % per) * narrow + start, LANES)
            weights = reduce[owner // per, :, pl.ds(at_lane, size)]
        else:
            weights = reduce[owner]
        return dot(hidden[at(half, t), :], weights)

    def grad_part(half, t, owner, start, size):
        at_row = pl.multiple_of((owner % per) * narrow + start, 16)
        return turned(slopes[at(half, t), :], expand[owner // per, pl.ds(at_row, size), :])

    def emit_branch(t, rows_at, span, start, size, value):
        lane = slice(start, start + size)
        value = scale[:, lane] * (value + b_reduce[:, lane])
        held[rows_at, span] = (held[rows_at, span].astype(f32) + value).astype(bf16)

    def emit_grad(t, rows_at, span, start, size, value):
        lane = slice(start, start + size)
        mean, inv = stats[rows_at, 0:1], stats[rows_at, 1:2]
        both = jnp.transpose(sums[0, t])
        normal = (mixed[rows_at, span].astype(f32) - mean) * inv
        value = value * local_gain[:, lane]
        value = inv * (value - both[:, 0:1] / channels - normal * both[:, 1:2] / channels)
        mixed[rows_at, span] = value.astype(bf16)

    def grad_tokens(t):
        @pl.loop(0, 2)
        def _(half):
            rows_at = pl.ds(pl.multiple_of(t * tile, 16), tile)
            value = jnp.zeros((tile, units), f32)
            for b in range(rows):
                group = [grads[half, b * per + i, rows_at, :] for i in range(per)]
                if sliced:
                    value += turned(jnp.concatenate(group, 1), reduce[b])
                else:
                    for i in range(per):
                        value += turned(group[i], reduce[b * per + i])
            a = preact[group_at(half, t)].reshape(tile, units)
            cumulative = 0.5 * (1.0 + lax.erf(a * root_half))
            slope = cumulative + a * jnp.exp(-0.5 * a * a) * density_scale
            rounded = (value * slope).astype(bf16)
            slopes[at(half, t), :] = rounded
            rounded = rounded.astype(f32)
            total = jnp.sum(rounded * units_in[0:1, :], 1, keepdims=True)
            cross = jnp.sum(rounded * (a - units_in[1:2, :]), 1, keepdims=True)
            lane = lax.broadcasted_iota(jnp.int32, (tile, LANES), 1)
            both = jnp.where(lane == 0, total, jnp.where(lane == 1, cross, 0.0))
            sums[half, t] = jnp.transpose(both)[0:8]

    pl.semaphore_wait(free.at[0], len(nearby))
    branch_units = []
    for index, (start, size) in enumerate(reduce_ranges):
        columns, where = (start, size), stage
        if index == len(reduce_ranges) - 1 and index >= 2:
            columns, where = (start, size, reduce_ranges[0][0]), mixes.at[0]
        branch_units.append(
            sum_part(mixes, branch_part, columns, (0, tiles), emit_branch, where)
        )
    first_index, turn, across_index, last_index = 0, 1, 1 + steps, 2 + steps
    spare = len(branch_units) >= 3
    arrive(reduce_copies[0])
    for index, unit in enumerate(branch_units):
        if index:
            arrive(reduce_copies[index])
            before = branch_units[index - 1]
            for s in range(1, steps):
                before[turn + s]()
            if spare and index == len(branch_units) - 1:
                for done in branch_units[: index - 1]:
                    done[last_index]()
        unit[first_index]()
        if index:
            before[across_index]()
        unit[turn]()

    arrive_core(grad_core, 0)
    arrive_core(grad_core, 1)
    leave_gather(grad_steps, grad_across, grad_core)
    latest = branch_units[-1]
    for unit in branch_units[:-1]:
        unit[-1]()

    def finish_latest():
        for s in range(1, steps):
            latest[turn + s]()

    sum_devices = [partner] + [(r, flip(c, bit)) for bit in [1] + bits]
    sum_copies = [
        remote(sums.at[1 if n == 0 else 0], sums_in.at[n], new(), device)
        for n, device in enumerate(sum_devices)
    ]

    def sum_step(n):
        if 0 < n <= len(sum_copies):
            sum_copies[n - 1].wait()
            sums[0] = sums[0] + sums_in[n - 1]
        if n < len(sum_copies):
            sum_copies[n].start()

    grad_units = [sum_part(grads, grad_part, (0, narrow), (t, 1), emit_grad) for t in range(tiles)]

    if not spare:
        finish_latest()
        latest[across_index]()
        latest[-1]()
    for t, unit in enumerate(grad_units):
        grad_tokens(t)
        release(1 + t)
        if t == tiles - 1:
            sum_step(0)
        pl.semaphore_wait(free.at[1 + t], len(nearby))
        unit[first_index]()
        unit[turn]()
        if spare and t == 0:
            finish_latest()
        if spare and t == min(1, tiles - 1):
            latest[across_index]()
    sum_index = 1
    for t, unit in enumerate(grad_units):
        for s in range(1, steps):
            unit[turn + s]()
        if t:
            grad_units[t - 1][across_index]()
        sum_step(sum_index)
        sum_index += 1
    grad_units[-1][across_index]()
    while sum_index <= len(sum_copies):
        sum_step(sum_index)
        sum_index += 1
    for unit in branch_units[-2:] if spare else branch_units:
        unit[last_index]()
    out_copy = pltpu.make_async_copy(held, out, local.at[0])
    out_copy.start()
    for unit in grad_units:
        unit[last_index]()
    grad_copy = pltpu.make_async_copy(mixed, grad_mixed, local.at[1])
    grad_copy.start()
    if spare:
        latest[-1]()
    for unit in grad_units:
        unit[-1]()
    out_copy.wait()
    grad_copy.wait()

    leave(expand_copies)
    for copies in reduce_copies:
        leave(copies)
    if per_image > 1:
        pl.when(has_bottom)(down.wait_send)
        pl.when(has_top)(up.wait_send)


def semaphores_needed(rows, cols, per, reduce_parts, grad_parts):
    blocks, steps = cols // 2, cols.bit_length() - 2
    gathers = 4 * (2 * (blocks - 1) + 1 + 2 * blocks)
    weights = (rows - 1) * (1 + per * reduce_parts)
    return 2 + weights + gathers + (reduce_parts + grad_parts) * (4 * blocks - 1) + steps + 2


def body(
    activations,
    cotangent,
    kernel,
    ln_gain,
    ln_bias,
    w_expand,
    b_expand,
    w_reduce,
    b_reduce,
    layer_scale,
):
    row_count, grid_width, narrow = activations.shape
    rows, cols = lax.axis_size("row"), lax.axis_size("col")
    me_row, me_col = lax.axis_index("row"), lax.axis_index("col")
    channels = narrow * cols
    depth = channels // rows
    per = depth // narrow
    tokens = row_count * grid_width
    units = w_expand.shape[1] // 2
    sliced = narrow % LANES == 0
    tile = token_tile(tokens)
    f32, bf16 = jnp.float32, jnp.bfloat16

    cot_f = cotangent.astype(f32)
    grad_branch = (layer_scale * cot_f).reshape(tokens, narrow).astype(bf16)
    bias = lax.dynamic_slice_in_dim(b_expand, (me_row % 2) * units, units)[None, :]
    if sliced:
        reduce_source = w_reduce
        reduce_shape = (rows, units, depth)
    else:
        reduce_source = w_reduce.reshape(2, units, per, narrow).transpose(0, 2, 1, 3)
        reduce_shape = (cols, units, narrow)
    local_gain = lax.dynamic_slice_in_dim(ln_gain, me_col * narrow, narrow)
    reduce_parts = len(split_columns(narrow))
    count = semaphores_needed(rows, cols, per, reduce_parts, tokens // tile)
    steps = cols.bit_length() - 2

    anywhere = pl.BlockSpec(memory_space=pl.ANY)
    inside = pl.BlockSpec(memory_space=pltpu.VMEM)
    flops = 8 * 2 * tokens * channels * units
    block_out, grad_mixed = pl.pallas_call(
        functools.partial(block_kernel, rows, cols),
        out_shape=[jax.ShapeDtypeStruct((tokens, narrow), bf16)] * 2,
        in_specs=[anywhere] * 4 + [inside] * 7,
        out_specs=[anywhere] * 2,
        scratch_shapes=[
            pltpu.VMEM((2, cols, tokens, narrow), bf16),
            pltpu.VMEM((2, cols, tokens, narrow), bf16),
            pltpu.VMEM((cols, tokens, narrow), bf16),
            pltpu.VMEM((tokens, narrow), bf16),
            pltpu.VMEM((rows, depth, units), bf16),
            pltpu.VMEM(reduce_shape, bf16),
            pltpu.VMEM((2 * tokens, units), bf16),
            pltpu.VMEM((2 * tokens, units), bf16),
            pltpu.VMEM((2 * tokens // (grid_width + 16), grid_width + 16, units), f32),
            pltpu.VMEM((tokens, narrow), bf16),
            pltpu.VMEM((tokens, 2), f32),
            pltpu.VMEM((2, units), f32),
            pltpu.VMEM((2, tokens // tile, 8, tile), f32),
            pltpu.VMEM((steps + 2, tokens // tile, 8, tile), f32),
            pltpu.VMEM((3 * grid_width, narrow), bf16),
            pltpu.VMEM((3 * grid_width, narrow), bf16),
            pltpu.SemaphoreType.DMA((count,)),
            pltpu.SemaphoreType.DMA((count,)),
            pltpu.SemaphoreType.DMA((5 + per * reduce_parts,)),
            pltpu.SemaphoreType.REGULAR((1 + tokens // tile,)),
        ],
        compiler_params=pltpu.CompilerParams(
            collective_id=0, has_side_effects=True, vmem_limit_bytes=VMEM_LIMIT
        ),
        cost_estimate=pl.CostEstimate(
            flops=flops, bytes_accessed=8 * channels * units, transcendentals=0
        ),
        name="block",
    )(
        activations.reshape(tokens, narrow),
        grad_branch,
        w_expand,
        reduce_source,
        kernel,
        bias,
        ln_gain.reshape(cols, 1, narrow),
        ln_bias.reshape(cols, 1, narrow),
        local_gain[None, :],
        layer_scale[None, :],
        b_reduce[None, :],
    )
    grad_mixed = grad_mixed.reshape(row_count, grid_width, narrow)
    top, bottom = halo(grad_mixed)
    grad_input = depthwise(grad_mixed, top, bottom, kernel, True, cotangent)
    return (block_out.reshape(row_count, grid_width, narrow), grad_input)


def solution(mesh):
    return jax.shard_map(
        body,
        mesh=mesh,
        in_specs=(
            P("row", None, "col"),
            P("row", None, "col"),
            P(None, None, "col"),
            P(),
            P(),
            P("row", "col"),
            P("col"),
            P("col", "row"),
            P("col"),
            P("col"),
        ),
        out_specs=(P("row", None, "col"), P("row", None, "col")),
        check_vma=False,
    )
```

```python
import functools

import jax
import jax.numpy as jnp
from jax import lax
from jax.experimental import pallas as pl
from jax.experimental.pallas import tpu as pltpu
from jax.sharding import PartitionSpec as P

H = 48
LANES = 128

epsilon = 1e-06
root_half = 0.7071067811865476
density_scale = 0.3989422804014327


def conv_kernel(flip, add, x_ref, top_ref, bottom_ref, k_ref, *rest):
    if add:
        add_ref, o_ref, field = rest
    else:
        o_ref, field = rest
    rows, width, lanes = x_ref.shape
    field[...] = jnp.zeros_like(field)
    field[0:3, 8 : 8 + width, :] = top_ref[...].astype(jnp.float32)
    field[3 : 3 + rows, 8 : 8 + width, :] = x_ref[...].astype(jnp.float32)
    field[3 + rows : 6 + rows, 8 : 8 + width, :] = bottom_ref[...].astype(jnp.float32)

    @pl.loop(0, rows)
    def _(r):
        total = jnp.zeros((width, lanes), jnp.float32)
        for a in range(7):
            for b in range(7):
                weight = k_ref[6 - a, 6 - b] if flip else k_ref[a, b]
                total += weight[None, :] * field[r + a, 5 + b : 5 + b + width, :]
        mixed = total.astype(jnp.bfloat16)
        if add:
            mixed = (add_ref[r].astype(jnp.float32) + mixed.astype(jnp.float32)).astype(
                jnp.bfloat16
            )
        o_ref[r] = mixed


def depthwise(field, top, bottom, kernel, flip, add=None):
    rows, width, channels = field.shape
    lanes = LANES if channels % LANES == 0 else channels
    block = lambda n: pl.BlockSpec((n, width, lanes), lambda i: (0, 0, i))
    operands = [field, top, bottom, kernel]
    specs = [block(rows), block(3), block(3), pl.BlockSpec((7, 7, lanes), lambda i: (0, 0, i))]
    if add is not None:
        operands.append(add)
        specs.append(block(rows))
    return pl.pallas_call(
        functools.partial(conv_kernel, flip, add is not None),
        out_shape=jax.ShapeDtypeStruct(field.shape, jnp.bfloat16),
        grid=(channels // lanes,),
        in_specs=specs,
        out_specs=block(rows),
        scratch_shapes=[pltpu.VMEM((rows + 6, width + 16, lanes), jnp.float32)],
        compiler_params=pltpu.CompilerParams(vmem_limit_bytes=32 * 2**20),
        cost_estimate=pl.CostEstimate(
            flops=98 * rows * width * channels,
            bytes_accessed=6 * rows * width * channels,
            transcendentals=0,
        ),
        name="depthwise_flipped" if flip else "depthwise",
    )(*operands)


def halo(field):
    rows = field.shape[0]
    per_image = H // rows
    count = lax.axis_size("row")
    down = [(i, i + 1) for i in range(count - 1) if (i + 1) % per_image]
    up = [(j, i) for i, j in down]
    return lax.ppermute(field[-3:], "row", down), lax.ppermute(field[:3], "row", up)


MESH = pl.DeviceIdType.MESH
VMEM_LIMIT = 127 * 2**19


def flip(index, bit):
    return index + bit - 2 * bit * ((index // bit) % 2)


def flip_all(index, mask):
    bit = 1
    while bit <= mask:
        if mask & bit:
            index = flip(index, bit)
        bit *= 2
    return index


def token_tile(tokens):
    for tile in (384, 192, 96, 48, 16):
        if tokens % tile == 0:
            return tile
    return tokens


def split_columns(narrow):
    if narrow % LANES:
        return [(0, narrow)]
    return [(start, LANES) for start in range(0, narrow, LANES)]


def block_kernel(
    rows,
    cols,
    act,
    grad,
    w_expand,
    w_reduce,
    taps,
    bias,
    gain,
    shift,
    scale,
    b_reduce,
    out,
    grad_mixed,
    mixes,
    grads,
    stage,
    held,
    expand,
    reduce,
    hidden,
    slopes,
    preact,
    mixed,
    stats,
    units_in,
    sums,
    sums_in,
    top,
    bottom,
    send,
    recv,
    local,
    free,
):
    tokens, narrow = grad.shape
    width = top.shape[0] // 3
    row_count = tokens // width
    channels = narrow * cols
    depth, units = expand.shape[1:]
    per = depth // narrow
    sliced = narrow % LANES == 0
    tile = token_tile(tokens)
    tiles = tokens // tile
    small = min(tile, 192)
    per_image = H // row_count
    r, c = lax.axis_index("row"), lax.axis_index("col")
    parity = r % 2
    blocks = cols // 2
    bits = [1 << b for b in range(1, cols.bit_length() - 1)]
    steps = len(bits)
    second = bits[steps // 2 :] + bits[: steps // 2]
    f32, bf16 = jnp.float32, jnp.bfloat16
    dot = functools.partial(jnp.dot, preferred_element_type=f32)
    turned = lambda left, right: lax.dot_general(
        left, right, (((1,), (1,)), ((), ())), preferred_element_type=f32
    )
    row_of = lambda distance: (flip_all(r, distance), c)
    core = (r, flip(c, 1))
    partner = row_of(1)

    def step_column(index, half, s):
        e = (r + half) % 2
        return flip(index, bits[s]) * (1 - e) + flip(index, second[s]) * e

    def owner_of(half, j):
        index = c
        for s in range(steps):
            index = index + ((j // (1 << s)) % 2) * (step_column(index, half, s) - index)
        return index

    counter = [0]

    def new(count=1):
        counter[0] += count
        return counter[0] - count

    def remote(src, dst, sem, device):
        return pltpu.make_async_remote_copy(
            src_ref=src,
            dst_ref=dst,
            send_sem=send.at[sem],
            recv_sem=recv.at[sem],
            device_id=device,
            device_id_type=MESH,
        )

    barrier = pltpu.get_barrier_semaphore()
    others = [row_of(d) for d in range(1, rows)] + [(r, flip(c, bit)) for bit in [1] + bits]
    for device in others:
        pl.semaphore_signal(barrier, inc=1, device_id=device, device_id_type=MESH)
    pl.semaphore_wait(barrier, len(others))

    has_top, has_bottom = r % per_image != 0, (r + 1) % per_image != 0
    up_device = ((r + rows - 1) % rows, c)
    down_device = ((r + 1) % rows, c)
    down = remote(act.at[pl.ds(tokens - 3 * width, 3 * width)], top, new(), down_device)
    up = remote(act.at[pl.ds(0, 3 * width)], bottom, new(), up_device)
    if per_image > 1:
        pl.when(has_bottom)(down.start)
        pl.when(has_top)(up.start)

    def parts_of_expand(distance):
        half = (flip_all(r, distance) % 2) * units
        return w_expand.at[:, pl.ds(pl.multiple_of(half, units), units)]

    reduce_ranges = split_columns(narrow)

    def parts_of_reduce(distance, start, size):
        half = flip_all(r, distance) % 2
        pairs = []
        for i in range(per):
            if sliced:
                span = pl.ds(i * narrow + start, size)
                rows_of = pl.ds(pl.multiple_of(half * units, units), units)
                pairs.append((w_reduce.at[rows_of, span], reduce.at[r, :, span]))
            else:
                pairs.append((w_reduce.at[half, i], reduce.at[r * per + i]))
        return pairs

    def loads(pairs, base):
        copies = []
        for index, (src, dst) in enumerate(pairs):
            copies.append(pltpu.make_async_copy(src, dst, local.at[base + index]))
            copies[-1].start()
        return copies

    act_in = loads([(act, held)], 0)
    expand_own = loads([(parts_of_expand(0), expand.at[r])], 3)
    grad_own = loads([(grad, grads.at[0, c])], 4)

    expand_copies = [
        remote(parts_of_expand(d), expand.at[r], new(), row_of(d)) for d in range(rows - 1, 0, -1)
    ]

    sets = 2
    set_tokens = tokens // sets

    def gather(buffer, source):
        def there(half, j, q):
            span = pl.ds(q * set_tokens, set_tokens)
            order = (bits, second)[q]
            owner = c
            for s in range(steps):
                if (j >> s) & 1:
                    owner = flip(owner, order[s])
            target = buffer.at[half, owner, span]
            return (source.at[span] if half == 0 and j == 0 else target), target

        def step_copies(half, s, q):
            device = (r, flip(c, (bits, second)[q][s]))
            return [remote(*there(half, j, q), new(), device) for j in range(1 << s)]

        step_list = [
            [[step_copies(half, s, q) for q in range(sets)] for s in range(steps)]
            for half in (0, 1)
        ]
        across = []
        for q in range(sets):
            span = pl.ds(q * set_tokens, set_tokens)
            across.append(remote(source.at[span], buffer.at[1, c, span], new(), partner))
        core_list = [
            [[remote(*there(half, j, q), new(), core) for j in range(blocks)] for q in range(sets)]
            for half in (0, 1)
        ]
        return step_list, across, core_list

    grad_steps, grad_across, grad_core = gather(grads, grad)
    mix_steps, mix_across, mix_core = gather(mixes, mixed)

    reduce_copies = []
    for start, size in reduce_ranges:
        copies = []
        for d in range(rows - 1, 0, -1):
            copies += [
                remote(src, dst, new(), row_of(d)) for src, dst in parts_of_reduce(d, start, size)
            ]
        reduce_copies.append(copies)

    def begin(copies):
        for copy in copies:
            copy.start()

    def arrive(copies):
        for copy in copies:
            copy.wait_recv()

    def leave(copies):
        for copy in copies:
            copy.wait_send()

    for q in range(sets):
        begin(grad_steps[0][0][q])
    begin(expand_copies[:1])
    reduce_own = loads(
        [pair for start, size in reduce_ranges for pair in parts_of_reduce(0, start, size)], 5
    )

    for copy in act_in:
        copy.wait()
    if per_image > 1:

        @pl.when(has_top)
        def _():
            down.wait_recv()

        @pl.when(has_bottom)
        def _():
            up.wait_recv()

    lanes = LANES if sliced else narrow
    pitch = preact.shape[1]

    def place(row, value):
        preact[row, 8 : 8 + width, 0:lanes] = value.astype(f32)

    for group in range(narrow // lanes):
        span = pl.ds(group * lanes, lanes)

        @pl.loop(0, row_count + 6)
        def _(i):
            preact[i, :, 0:lanes] = jnp.zeros((pitch, lanes), f32)

        @pl.loop(0, row_count)
        def _(i):
            place(i + 3, held[pl.ds(pl.multiple_of(i * width, 16), width), span])

        if per_image > 1:

            @pl.when(has_top)
            def _():
                for i in range(3):
                    place(i, top[i * width : (i + 1) * width, span])

            @pl.when(has_bottom)
            def _():
                for i in range(3):
                    place(i + row_count + 3, bottom[i * width : (i + 1) * width, span])

        @pl.loop(0, row_count)
        def _(i):
            total = jnp.zeros((width, lanes), f32)
            for a in range(7):
                for b in range(7):
                    total += (
                        taps[a, b, span][None, :]
                        * preact[i + a, 5 + b : 5 + b + width, 0:lanes]
                    )
            value = total.astype(bf16)
            mixed[pl.ds(pl.multiple_of(i * width, 16), width), span] = value

    begin(mix_across)
    for q in range(sets):
        begin(mix_steps[0][0][q])
    own_mixed = loads([(mixed, mixes.at[0, c])], 1)
    for q in range(sets):
        begin(mix_core[0][q][:1])
    for copy in own_mixed + grad_own:
        copy.wait()

    def advance(step_list, core_list, half, s):
        for q in range(sets):
            arrive(step_list[half][s][q])
            if s + 1 < steps:
                begin(step_list[half][s + 1][q])
            begin(core_list[half][q][1 << s : 2 << s])

    advance(mix_steps, mix_core, 0, 0)
    for q in range(sets):
        arrive(mix_across[q : q + 1])
        begin(mix_steps[1][0][q])
        begin(mix_core[1][q][:1])
        if q == 0:
            begin(expand_copies[1:-1])
    begin(grad_across)
    begin(expand_copies[-1:])
    for s in range(1, steps):
        advance(mix_steps, mix_core, 0, s)
        advance(mix_steps, mix_core, 1, s - 1)
    advance(mix_steps, mix_core, 1, steps - 1)
    advance(grad_steps, grad_core, 0, 0)
    for q in range(sets):
        begin(grad_core[0][q][:1])
    for q in range(sets):
        arrive(grad_across[q : q + 1])
        begin(grad_steps[1][0][q])
        begin(grad_core[1][q][:1])
    for copy in reduce_own + expand_own:
        copy.wait()
    begin(reduce_copies[0])
    arrive(expand_copies)

    extra = jnp.zeros((16, units), f32)
    for o in range(cols):
        exact = []
        for vector in (gain[o], shift[o]):
            for _ in range(3):
                piece = vector.astype(bf16).astype(f32)
                exact.append(piece)
                vector = vector - piece
        exact.append(jnp.zeros((16 - len(exact), narrow), f32))
        exact = jnp.concatenate(exact, 0).astype(bf16)
        lane = (o % per) * narrow
        extra += dot(exact, expand[o // per, lane : lane + narrow, :])
    units_in[0:1, :] = extra[0:1] + extra[1:2] + extra[2:3]
    units_in[1:2, :] = bias[parity] + (extra[3:4] + extra[4:5] + extra[5:6])

    def at(half, t, tile=tile):
        return pl.ds(pl.multiple_of(half * tokens + t * tile, 16), tile)

    def group_at(half, t, tile=tile):
        return pl.ds(half * (tokens // pitch) + t * (tile // pitch), tile // pitch)

    def expand_tokens(half):
        @pl.loop(0, tokens // small)
        def _(t):
            rows_at = pl.ds(pl.multiple_of(t * small, 16), small)
            total = jnp.zeros((small, 1), f32)
            square = jnp.zeros((small, 1), f32)
            for o in range(cols):
                value = mixes[half, o, rows_at, :].astype(f32)
                total += jnp.sum(value, 1, keepdims=True)
                square += jnp.sum(value * value, 1, keepdims=True)
            mean = total / channels
            inv = lax.rsqrt(square / channels - mean * mean + epsilon)
            if half == 0:
                stats[rows_at, 0:1] = mean
                stats[rows_at, 1:2] = inv
            value = jnp.zeros((small, units), f32) + bias[parity]
            for b in range(rows):
                group = [b * per + i for i in range(per)]
                normed = [
                    (
                        (mixes[half, o, rows_at, :].astype(f32) - mean) * inv * gain[o] + shift[o]
                    ).astype(bf16)
                    for o in group
                ]
                if sliced:
                    value += dot(jnp.concatenate(normed, 1), expand[b])
                else:
                    for i in range(per):
                        value += dot(normed[i], expand[b, i * narrow : (i + 1) * narrow, :])
            cumulative = 0.5 * (1.0 + lax.erf(value * root_half))
            hidden[at(half, t, small), :] = (value * cumulative).astype(bf16)
            preact[group_at(half, t, small)] = value.reshape(-1, pitch, units)

    def arrive_core(core_list, half):
        for q in range(sets):
            arrive(core_list[half][q])

    arrive_core(mix_core, 0)
    expand_tokens(0)
    for copies in reduce_copies[1:2]:
        begin(copies)
    for s in range(1, steps):
        advance(grad_steps, grad_core, 0, s)
    advance(grad_steps, grad_core, 1, 0)
    arrive_core(mix_core, 1)
    expand_tokens(1)
    for copies in reduce_copies[2:]:
        begin(copies)
    for s in range(1, steps):
        advance(grad_steps, grad_core, 1, s)

    nearby = [core, partner] + [(r, flip(c, bit)) for bit in bits]

    def release(index):
        for device in nearby:
            pl.semaphore_signal(free.at[index], inc=1, device_id=device, device_id_type=MESH)

    def leave_gather(step_list, across, core_list):
        leave(across)
        for half in (0, 1):
            for q in range(sets):
                leave(core_list[half][q])
                for s in range(steps):
                    leave(step_list[half][s][q])

    leave_gather(mix_steps, mix_across, mix_core)
    release(0)

    def sum_part(buffer, part, columns, tile_range, emit, stage=stage):
        base = new(4 * blocks - 1)
        start, size = columns[:2]
        span = pl.ds(start, size)
        stage_span = pl.ds(columns[-1] if len(columns) > 2 else start, size)
        first_tile, tile_count = tile_range
        here = pl.ds(first_tile * tile, tile_count * tile)

        def core_copy(half, j, slot):
            return remote(
                stage.at[slot, here, stage_span],
                buffer.at[half, j, here, span],
                base + half * blocks + j,
                core,
            )

        def step_copy(half, s, i):
            return remote(
                stage.at[2 * ((1 << s) - 1) + 2 * i + half, here, stage_span],
                buffer.at[half, blocks + (1 << s) - 1 + i, here, span],
                base + 2 * blocks + 2 * ((1 << s) - 1) + 2 * i + half,
                (r, step_column(c, half, s)),
            )

        pair_copy = remote(
            stage.at[2 * (blocks - 1), here, stage_span],
            buffer.at[0, cols - 1, here, span],
            base + 4 * blocks - 2,
            partner,
        )

        def total(half, t, owner, j, later):
            rows_at = pl.ds(pl.multiple_of(t * tile, 16), tile)
            value = part(half, t, owner, start, size)
            value += buffer[half, j, rows_at, span].astype(f32)
            for s in later:
                value += buffer[half, blocks + (1 << s) - 1 + j, rows_at, span].astype(f32)
            return value

        def over_tiles(slot, value_of):
            @pl.loop(first_tile, first_tile + tile_count)
            def _(t):
                rows_at = pl.ds(pl.multiple_of(t * tile, 16), tile)
                stage[slot, rows_at, stage_span] = value_of(t).astype(bf16)

        def first():
            @pl.loop(0, 2 * blocks)
            def _(i):
                half, j = i % 2, blocks - 1 - i // 2
                owner = flip(owner_of(half, j), 1)
                over_tiles(i, lambda t: part(half, t, owner, start, size))
                core_copy(half, j, i).start()

        def clear():
            @pl.loop(0, 2 * blocks)
            def _(i):
                core_copy(i % 2, blocks - 1 - i // 2, i).wait_send()

        def step(s):
            @pl.loop(0, 2 << s)
            def _(n):
                half, i = n % 2, n // 2
                j = i + (1 << s)
                core_copy(half, j, 0).wait_recv()
                for later in range(s + 1, steps):
                    step_copy(half, later, j).wait_recv()
                owner = owner_of(half, j)
                over_tiles(
                    2 * ((1 << s) - 1) + n,
                    lambda t: total(half, t, owner, j, range(s + 1, steps)),
                )
                step_copy(half, s, i).start()

        def across():
            core_copy(1, 0, 0).wait_recv()
            for s in range(steps):
                step_copy(1, s, 0).wait_recv()
            over_tiles(2 * (blocks - 1), lambda t: total(1, t, c, 0, range(steps)))
            pair_copy.start()

        def last():
            core_copy(0, 0, 0).wait_recv()
            for s in range(steps):
                step_copy(0, s, 0).wait_recv()
            pair_copy.wait_recv()

            @pl.loop(first_tile, first_tile + tile_count)
            def _(t):
                rows_at = pl.ds(pl.multiple_of(t * tile, 16), tile)
                value = total(0, t, c, 0, range(steps))
                value += buffer[0, cols - 1, rows_at, span].astype(f32)
                emit(t, rows_at, span, start, size, value)

        def finish():
            for s in range(steps):

                @pl.loop(0, 2 << s)
                def _(n):
                    step_copy(n % 2, s, n // 2).wait_send()

            pair_copy.wait_send()

        def step_cleared(s):
            if s == steps - 1:
                clear()
            step(s)

        turns = [functools.partial(step_cleared, s) for s in range(steps - 1, -1, -1)]
        return [first] + turns + [across, last, finish]

    def branch_part(half, t, owner, start, size):
        if sliced:
            at_lane = pl.multiple_of((owner % per) * narrow + start, LANES)
            weights = reduce[owner // per, :, pl.ds(at_lane, size)]
        else:
            weights = reduce[owner]
        return dot(hidden[at(half, t), :], weights)

    def grad_part(half, t, owner, start, size):
        at_row = pl.multiple_of((owner % per) * narrow + start, 16)
        return turned(slopes[at(half, t), :], expand[owner // per, pl.ds(at_row, size), :])

    def emit_branch(t, rows_at, span, start, size, value):
        lane = slice(start, start + size)
        value = scale[lane][None, :] * (value + b_reduce[lane][None, :])
        held[rows_at, span] = (held[rows_at, span].astype(f32) + value).astype(bf16)

    def emit_grad(t, rows_at, span, start, size, value):
        lane = slice(start, start + size)
        mean, inv = stats[rows_at, 0:1], stats[rows_at, 1:2]
        both = jnp.transpose(sums[0, t])
        normal = (mixed[rows_at, span].astype(f32) - mean) * inv
        value = value * gain[c, :, lane]
        value = inv * (value - both[:, 0:1] / channels - normal * both[:, 1:2] / channels)
        mixed[rows_at, span] = value.astype(bf16)

    def grad_tokens(t):
        @pl.loop(0, 2)
        def _(half):
            rows_at = pl.ds(pl.multiple_of(t * tile, 16), tile)
            value = jnp.zeros((tile, units), f32)
            for b in range(rows):
                group = [grads[half, b * per + i, rows_at, :] for i in range(per)]
                if sliced:
                    value += turned(jnp.concatenate(group, 1), reduce[b])
                else:
                    for i in range(per):
                        value += turned(group[i], reduce[b * per + i])
            a = preact[group_at(half, t)].reshape(tile, units)
            cumulative = 0.5 * (1.0 + lax.erf(a * root_half))
            slope = cumulative + a * jnp.exp(-0.5 * a * a) * density_scale
            rounded = (value * slope).astype(bf16)
            slopes[at(half, t), :] = rounded
            rounded = rounded.astype(f32)
            total = jnp.sum(rounded * units_in[0:1, :], 1, keepdims=True)
            cross = jnp.sum(rounded * (a - units_in[1:2, :]), 1, keepdims=True)
            lane = lax.broadcasted_iota(jnp.int32, (tile, LANES), 1)
            both = jnp.where(lane == 0, total, jnp.where(lane == 1, cross, 0.0))
            sums[half, t] = jnp.transpose(both)[0:8]

    pl.semaphore_wait(free.at[0], len(nearby))
    branch_units = []
    for index, (start, size) in enumerate(reduce_ranges):
        columns, where = (start, size), stage
        if index == len(reduce_ranges) - 1 and index >= 2:
            columns, where = (start, size, reduce_ranges[0][0]), mixes.at[0]
        branch_units.append(
            sum_part(mixes, branch_part, columns, (0, tiles), emit_branch, where)
        )
    first_index, turn, across_index, last_index = 0, 1, 1 + steps, 2 + steps
    spare = len(branch_units) >= 3
    arrive(reduce_copies[0])
    for index, unit in enumerate(branch_units):
        if index:
            arrive(reduce_copies[index])
            before = branch_units[index - 1]
            for s in range(1, steps):
                before[turn + s]()
            if spare and index == len(branch_units) - 1:
                for done in branch_units[: index - 1]:
                    done[last_index]()
        unit[first_index]()
        if index:
            before[across_index]()
        unit[turn]()

    arrive_core(grad_core, 0)
    arrive_core(grad_core, 1)
    leave_gather(grad_steps, grad_across, grad_core)
    latest = branch_units[-1]
    for unit in branch_units[:-1]:
        unit[-1]()

    def finish_latest():
        for s in range(1, steps):
            latest[turn + s]()

    sum_devices = [partner] + [(r, flip(c, bit)) for bit in [1] + bits]
    sum_copies = [
        remote(sums.at[1 if n == 0 else 0], sums_in.at[n], new(), device)
        for n, device in enumerate(sum_devices)
    ]

    def sum_step(n):
        if 0 < n <= len(sum_copies):
            sum_copies[n - 1].wait()
            sums[0] = sums[0] + sums_in[n - 1]
        if n < len(sum_copies):
            sum_copies[n].start()

    grad_units = [sum_part(grads, grad_part, (0, narrow), (t, 1), emit_grad) for t in range(tiles)]

    if not spare:
        finish_latest()
        latest[across_index]()
        latest[-1]()
    for t, unit in enumerate(grad_units):
        grad_tokens(t)
        release(1 + t)
        if t == tiles - 1:
            sum_step(0)
        pl.semaphore_wait(free.at[1 + t], len(nearby))
        unit[first_index]()
        unit[turn]()
        if spare and t == 0:
            finish_latest()
        if spare and t == min(1, tiles - 1):
            latest[across_index]()
    sum_index = 1
    for t, unit in enumerate(grad_units):
        for s in range(1, steps):
            unit[turn + s]()
        if t:
            grad_units[t - 1][across_index]()
        sum_step(sum_index)
        sum_index += 1
    grad_units[-1][across_index]()
    while sum_index <= len(sum_copies):
        sum_step(sum_index)
        sum_index += 1
    for unit in branch_units[-2:] if spare else branch_units:
        unit[last_index]()
    out_copy = pltpu.make_async_copy(held, out, local.at[0])
    out_copy.start()
    for unit in grad_units:
        unit[last_index]()
    grad_copy = pltpu.make_async_copy(mixed, grad_mixed, local.at[1])
    grad_copy.start()
    if spare:
        latest[-1]()
    for unit in grad_units:
        unit[-1]()
    out_copy.wait()
    grad_copy.wait()

    leave(expand_copies)
    for copies in reduce_copies:
        leave(copies)
    if per_image > 1:
        pl.when(has_bottom)(down.wait_send)
        pl.when(has_top)(up.wait_send)


def semaphores_needed(rows, cols, per, reduce_parts, grad_parts):
    blocks, steps = cols // 2, cols.bit_length() - 2
    gathers = 4 * (2 * (blocks - 1) + 1 + 2 * blocks)
    weights = (rows - 1) * (1 + per * reduce_parts)
    return 2 + weights + gathers + (reduce_parts + grad_parts) * (4 * blocks - 1) + steps + 2


def body(
    activations,
    cotangent,
    kernel,
    ln_gain,
    ln_bias,
    w_expand,
    b_expand,
    w_reduce,
    b_reduce,
    layer_scale,
):
    row_count, grid_width, narrow = activations.shape
    rows, cols = lax.axis_size("row"), lax.axis_size("col")
    channels = narrow * cols
    depth = channels // rows
    per = depth // narrow
    tokens = row_count * grid_width
    units = w_expand.shape[1] // 2
    sliced = narrow % LANES == 0
    tile = token_tile(tokens)
    f32, bf16 = jnp.float32, jnp.bfloat16

    cot_f = cotangent.astype(f32)
    grad_branch = (layer_scale * cot_f).reshape(tokens, narrow).astype(bf16)
    if sliced:
        reduce_source = w_reduce
        reduce_shape = (rows, units, depth)
    else:
        reduce_source = w_reduce.reshape(2, units, per, narrow).transpose(0, 2, 1, 3)
        reduce_shape = (cols, units, narrow)
    reduce_parts = len(split_columns(narrow))
    count = semaphores_needed(rows, cols, per, reduce_parts, tokens // tile)
    steps = cols.bit_length() - 2

    anywhere = pl.BlockSpec(memory_space=pl.ANY)
    inside = pl.BlockSpec(memory_space=pltpu.VMEM)
    flops = 8 * 2 * tokens * channels * units
    block_out, grad_mixed = pl.pallas_call(
        functools.partial(block_kernel, rows, cols),
        out_shape=[jax.ShapeDtypeStruct((tokens, narrow), bf16)] * 2,
        in_specs=[anywhere] * 4 + [inside] * 6,
        out_specs=[anywhere] * 2,
        scratch_shapes=[
            pltpu.VMEM((2, cols, tokens, narrow), bf16),
            pltpu.VMEM((2, cols, tokens, narrow), bf16),
            pltpu.VMEM((cols, tokens, narrow), bf16),
            pltpu.VMEM((tokens, narrow), bf16),
            pltpu.VMEM((rows, depth, units), bf16),
            pltpu.VMEM(reduce_shape, bf16),
            pltpu.VMEM((2 * tokens, units), bf16),
            pltpu.VMEM((2 * tokens, units), bf16),
            pltpu.VMEM((2 * tokens // (grid_width + 16), grid_width + 16, units), f32),
            pltpu.VMEM((tokens, narrow), bf16),
            pltpu.VMEM((tokens, 2), f32),
            pltpu.VMEM((2, units), f32),
            pltpu.VMEM((2, tokens // tile, 8, tile), f32),
            pltpu.VMEM((steps + 2, tokens // tile, 8, tile), f32),
            pltpu.VMEM((3 * grid_width, narrow), bf16),
            pltpu.VMEM((3 * grid_width, narrow), bf16),
            pltpu.SemaphoreType.DMA((count,)),
            pltpu.SemaphoreType.DMA((count,)),
            pltpu.SemaphoreType.DMA((5 + per * reduce_parts,)),
            pltpu.SemaphoreType.REGULAR((1 + tokens // tile,)),
        ],
        compiler_params=pltpu.CompilerParams(
            collective_id=0, has_side_effects=True, vmem_limit_bytes=VMEM_LIMIT
        ),
        cost_estimate=pl.CostEstimate(
            flops=flops, bytes_accessed=8 * channels * units, transcendentals=0
        ),
        name="block",
    )(
        activations.reshape(tokens, narrow),
        grad_branch,
        w_expand,
        reduce_source,
        kernel,
        b_expand.reshape(2, 1, units),
        ln_gain.reshape(cols, 1, narrow),
        ln_bias.reshape(cols, 1, narrow),
        layer_scale,
        b_reduce,
    )
    grad_mixed = grad_mixed.reshape(row_count, grid_width, narrow)
    top, bottom = halo(grad_mixed)
    grad_input = depthwise(grad_mixed, top, bottom, kernel, True, cotangent)
    return (block_out.reshape(row_count, grid_width, narrow), grad_input)


def solution(mesh):
    return jax.shard_map(
        body,
        mesh=mesh,
        in_specs=(
            P("row", None, "col"),
            P("row", None, "col"),
            P(None, None, "col"),
            P(),
            P(),
            P("row", "col"),
            P("col"),
            P("col", "row"),
            P("col"),
            P("col"),
        ),
        out_specs=(P("row", None, "col"), P("row", None, "col")),
        check_vma=False,
    )
```
